1024 devices in a mesh: grp: 64 (over z, core), tp: 16 (over y, x).
Axes of the slice: x: 4, y: 4, z: 32, core: 2. Of those that a mesh axis runs over, the one named last changes fastest.
Arguments:
- hidden: bfloat16 [24576, 5120], P('grp'), may hold values from -6 to 6
- merge_weight: bfloat16 [5120, 8192], P(None, 'tp'), may hold values from -0.078125 to 0.078125
- text_embed: bfloat16 [65536, 8192], P('grp', 'tp'), may hold values from -6 to 6
- gain: float32 [8192], P('tp'), may hold values from 0.1 to 1.9
- head_weight: float32 [8192, 19], P('tp'), may hold values from -2 to 2
- owner: int32 [24576, 1], P('grp'), may hold values from 0 to 63; in each aligned block of 384 rows (0 to 383, 384 to 767, ...) at most 12 rows name the same one
- vis_row: int32 [64, 768], P('grp'), may hold values from 0 to 1023, as said below
- lengths: int32 [64], P('grp'), may hold values from 256 to 1024
- labels: int32 [64, 19], replicated, may hold values from 0 to 1, as said below
- targets: float32 [64, 19], P('grp'), may hold values from -4 to 4
Outputs:
- reward: float32 [64, 19], P('grp')
- visual_grad: bfloat16 [24576, 8192], P('grp', 'tp')
- head_grad: float32 [8192, 19], P('tp')
- gain_grad: float32 [8192], P('tp')
The draws below stay inside these ranges and needn't reach their ends.
Inputs may be any that keep to these rules, and one draw needn't show every extreme that they name: `owner`: in each vision group's 384 rows no sample is named more than 12 times, a bound that some block reaches. `vis_row`: each row holds 768 different positions. `labels`: an objective may be rated by no sample.
All inputs are finite; a program needn't handle non-finite values.
Results may differ from the reference program's by a relative error of at most 0.0035.
Values may be sent and summed in bfloat16 or wider, within the bound.
No kernel may reach another device: no remote copies, remote signals or barrier semaphores. Data moves between devices by JAX's collectives and lax.ppermute only.
A program may use at most 64 MiB of HBM per device.

```python
import math
import jax
import jax.numpy as jnp
import numpy as np
from jax import lax

D = 8192
HM = 5120
K = 19
M_DEV = 384
S_DEV = 1024
SAMPLES = 64
VIS = 24576
CAP = 12
SLOTS = 768
ROWS = 65536
SCALE = 4096
N_GRP = 64


def draw_vis_row(key, part):
    keys = jax.random.split(jax.random.fold_in(key, 17), SAMPLES)

    def one_sample(sample_key):
        return jax.random.permutation(sample_key, S_DEV)[:SLOTS].astype(jnp.int32)
    return jax.vmap(one_sample)(keys)


def draw_labels(key, part):
    base = jax.random.fold_in(key, 29)
    mark_key, order_key, count_key = jax.random.split(base, 3)
    marks = (jax.random.randint(mark_key, (SAMPLES, K), 0, 4) == 0).astype(jnp.int32)
    order = jax.random.permutation(order_key, K).astype(jnp.int32)
    column_rank = jnp.zeros((K,), jnp.int32).at[order].set(jnp.arange(K, dtype=jnp.int32))
    cleared = jax.random.randint(count_key, (), 1, 3).astype(jnp.int32)
    keep = (column_rank >= cleared).astype(jnp.int32)
    return (marks * keep[None, :]).astype(jnp.int32)


def plant(array, stream_key, smallest, high):
    extent = array.shape
    place = [jax.random.randint(jax.random.fold_in(stream_key, axis), (), 0, extent[axis]) for axis in range(len(extent))]
    array = array.at[tuple(place)].set(smallest)
    longest = extent.index(max(extent))
    place[longest] = (place[longest] + 1) % extent[longest]
    return array.at[tuple(place)].set(high)


def levels(rng, dims, cuts, smallest, high):
    level, own = 1.0, jax.random.fold_in(rng, 6)
    for axis_at, shards_of in cuts:
        draws = jnp.exp(jax.random.uniform(jax.random.fold_in(own, axis_at), (shards_of,), jnp.float32, smallest / len(cuts), high / len(cuts)))
        level = level * jnp.repeat(draws, dims[axis_at] // shards_of).reshape([-1 if axis == axis_at else 1 for axis in range(len(dims))])
    return level


def deal_out(key, own, number, rows, amount, top, limit, slope):
    sequence = jax.random.permutation(key, amount)
    crowded, ordinary = shares(amount, rows * top, limit, slope, True), shares(amount, rows * top, limit, slope, False)
    places = jnp.arange(amount)

    def named(tallies, offset_by):
        used = int((tallies > 0).sum())
        fixed = max(1, used // 4)
        moved = fixed + (places - fixed + offset_by * (used - fixed)) % max(1, amount - fixed)
        return jnp.zeros((amount,), jnp.int32).at[sequence[jnp.where(places < fixed, places, moved)]].set(jnp.asarray(tallies, jnp.int32))

    tallies = jnp.where(number % 4 == 0, named(crowded, number // 4), named(ordinary, number - number // 4 - 1))
    mixed = jax.random.permutation(jax.random.fold_in(own, 3), amount)
    source_of, receiver = mixed[0:amount // 2 * 2:2], mixed[1:amount // 2 * 2:2]
    slack = jnp.minimum(tallies[source_of] - 1, limit - tallies[receiver]) // 2
    slack = jnp.where((source_of == sequence[0]) | (receiver == sequence[0]) | (tallies[receiver] == 0), 0, jnp.maximum(slack, 0))
    moved = jax.random.randint(jax.random.fold_in(own, 4), (amount // 2,), 0, 1 << 20) % (slack + 1)
    tallies = tallies.at[source_of].add(-moved).at[receiver].add(moved)
    items = jnp.searchsorted(jnp.cumsum(tallies), jnp.arange(rows * top), side="right").astype(jnp.int32)
    grid = items.reshape(top, rows).T
    grid = grid[jax.random.permutation(jax.random.fold_in(own, 1), rows)]
    offset_by = jax.random.randint(jax.random.fold_in(own, 2), (rows, 1), 0, top)
    return jnp.take_along_axis(grid, (jnp.arange(top)[None, :] + offset_by) % top, axis=1)


def shares(count, total, reach, slope, full):
    loads = [(1 << 20) // math.isqrt(grade ** slope) + 1 for grade in range(1, count + 1)]
    largest = reach if full else min(reach, max(-(-total // count), total * loads[0] // sum(loads)))
    least = 1 if total - largest >= count - 1 else 0
    given, surplus = [largest] + [least] * (count - 1), total - largest - least * (count - 1)
    while surplus > 0:
        movable = [i for i in range(1, count) if given[i] < largest] or [i for i in range(1, count) if given[i] < reach]
        whole, remaining = sum([loads[i] for i in movable]), surplus
        for i in movable:
            extra = min(reach - given[i], max(1, remaining * loads[i] // whole), surplus)
            given[i] = given[i] + extra
            surplus = surplus - extra
    return np.array(given)


def bell_draw(key, extent, spread, most, cuts=(), kind=jnp.bfloat16):
    loudness = levels(key, extent, cuts, -0.22, 0.18) if cuts else 1.0
    values = jax.random.normal(key, extent, jnp.float32) * spread * loudness
    return jnp.minimum(jnp.maximum(values, -most), most).astype(kind)


def setup_inputs(seed: int = 0) -> dict:
    arg_keys = jax.random.split(jax.random.key(seed), 11)
    hidden = bell_draw(arg_keys[0], (VIS, HM), 1.0, 6.0, ((0, 64),))
    merge_weight = bell_draw(arg_keys[1], (HM, D), HM ** -0.5, 0.078125, ((1, 16),))
    text_embed = bell_draw(arg_keys[2], (ROWS, D), 1.0, 6.0, ((0, 64), (1, 16)))
    gain = jnp.clip(1.0 + 0.18 * jax.random.normal(arg_keys[3], (D,), jnp.float32), 0.1, 1.9)
    head_weight = bell_draw(arg_keys[4], (D, K), (D // S_DEV) ** -0.5, 2.0, ((0, 16),), jnp.float32)
    owner_keys = jax.random.split(jax.random.fold_in(arg_keys[5], 1), VIS // M_DEV)
    owner_turns = jax.random.permutation(jax.random.fold_in(arg_keys[5], 3), VIS // M_DEV)
    owner = jax.vmap(lambda own, number: deal_out(jax.random.fold_in(arg_keys[5], 2), own, number, M_DEV, N_GRP, 1, CAP, 2))(owner_keys, owner_turns).reshape((VIS, 1))
    vis_row = draw_vis_row(jax.random.fold_in(arg_keys[10], 71), 0)
    lengths = plant(jax.random.randint(arg_keys[7], (SAMPLES,), S_DEV // 4, S_DEV + 1), jax.random.fold_in(arg_keys[7], 1), S_DEV // 4, S_DEV).astype(jnp.int32)
    labels = draw_labels(jax.random.fold_in(arg_keys[10], 71), 0)
    targets = bell_draw(arg_keys[9], (SAMPLES, K), 1.0, 4.0, ((0, 64),), jnp.float32)
    return {"hidden": hidden, "merge_weight": merge_weight, "text_embed": text_embed, "gain": gain, "head_weight": head_weight, "owner": owner, "vis_row": vis_row, "lengths": lengths, "labels": labels, "targets": targets}


epsilon = 1e-06

def reference(hidden, merge_weight, text_embed, gain, head_weight, owner, vis_row, lengths, labels, targets):
    visual = jnp.dot(hidden, merge_weight, preferred_element_type=jnp.float32).astype(jnp.bfloat16)
    owners = owner[:, 0].reshape(N_GRP, M_DEV).astype(jnp.int32)
    onehot = (owners[:, :, None] == jnp.arange(N_GRP, dtype=jnp.int32)[None, None, :]).astype(jnp.int32)
    slot_rank = (lax.optimization_barrier(jnp.sum(jnp.cumsum(onehot, axis=1) * onehot, axis=2)) - 1).astype(jnp.int32)
    slot_index = (jnp.arange(N_GRP, dtype=jnp.int32)[:, None] * CAP + slot_rank).astype(jnp.int32)
    local_row = vis_row[owners, slot_index].astype(jnp.int32)
    global_row = (owners * S_DEV + local_row).reshape(-1).astype(jnp.int32)
    placed = text_embed.at[global_row].set(visual)
    counts = lax.optimization_barrier(jnp.sum(labels.astype(jnp.float32), axis=0))

    def per_sample(item):
        sample_rows, length, marks, target = item
        xfull = sample_rows.astype(jnp.float32)
        row_sq = lax.optimization_barrier(jnp.sum(xfull * xfull, axis=1))
        inv_rms = lax.rsqrt(row_sq / D + epsilon)
        partial_value = jnp.dot(xfull * gain[None, :], head_weight, precision=lax.Precision.HIGHEST)
        live_rows = (jnp.arange(S_DEV, dtype=jnp.int32) < length).astype(jnp.float32)
        row_weight = live_rows * inv_rms / length.astype(jnp.float32)
        reward = lax.optimization_barrier(jnp.sum(row_weight[:, None] * partial_value, axis=0))
        cotangent = SCALE * marks.astype(jnp.float32) * (reward - target) / jnp.maximum(counts, 1.0)
        head_dir = jnp.dot(head_weight, cotangent, precision=lax.Precision.HIGHEST)
        row_dot = jnp.dot(partial_value, cotangent, precision=lax.Precision.HIGHEST)
        beta_row = row_weight * inv_rms * inv_rms * row_dot / D
        grad_rows = (row_weight[:, None] * (gain * head_dir)[None, :] - beta_row[:, None] * xfull).astype(jnp.bfloat16)
        pooled = lax.optimization_barrier(jnp.sum(row_weight[:, None] * xfull, axis=0))
        return (reward, grad_rows, jnp.outer(gain * pooled, cotangent), pooled * head_dir)
    rewards, grads, head_parts, gain_parts = lax.map(per_sample, (placed.reshape(SAMPLES, S_DEV, D), lengths, labels, targets))
    visual_grad = grads.reshape(-1, D)[global_row]
    return (rewards, visual_grad, lax.optimization_barrier(jnp.sum(head_parts, axis=0)), lax.optimization_barrier(jnp.sum(gain_parts, axis=0)))
```

```python
import functools

import jax
import jax.numpy as jnp
from jax import lax
from jax.experimental import pallas as pl
from jax.experimental.pallas import tpu as pltpu
from jax.sharding import Mesh
from jax.sharding import PartitionSpec as P

GRP = ("far", "near", "core")
NEAR = ("near", "core")
TP = ("ty", "tx")
EPSILON = 1e-06
LANES = 128
K_ROWS = 24
TARGET_AT = 32
VMEM = pltpu.CompilerParams(vmem_limit_bytes=48 * 2**20)
EXACT = lax.Precision.HIGHEST
LAST = (((1,), (1,)), ((), ()))
FIRST = (((0,), (0,)), ((), ()))


def iota(shape, dim):
    return lax.broadcasted_iota(jnp.int32, shape, dim)


def in_three(x):
    hi = x.astype(jnp.bfloat16)
    rest = x - hi.astype(jnp.float32)
    mid = rest.astype(jnp.bfloat16)
    return hi, mid, (rest - mid.astype(jnp.float32)).astype(jnp.bfloat16)


def dot32(a, b, dims):
    return lax.dot_general(a, b, dims, preferred_element_type=jnp.float32)


def dot_exact(a, b, dims):
    return lax.dot_general(a, b, dims, precision=EXACT, preferred_element_type=jnp.float32)


def flags_kernel(cap, length_ref, owner_ref, rows_ref, out_ref):
    groups = out_ref.shape[0]
    slots = rows_ref.shape[1]
    length = length_ref[0]
    live = (rows_ref[...] < length).astype(jnp.float32)
    slot = iota((groups, slots), 1)
    first = iota((groups, slots), 0) * cap
    mine = jnp.where((slot >= first) & (slot < first + cap), live, 0.0).astype(jnp.bfloat16)
    rank = lax.rem(iota((LANES, slots), 1), cap)
    place = (rank == iota((LANES, slots), 0)).astype(jnp.bfloat16)
    flags = dot32(mine, place, LAST)
    owned = (owner_ref[...] == iota((groups, owner_ref.shape[1]), 0)).astype(jnp.float32)
    count = jnp.sum(owned, axis=1, keepdims=True)
    lane = iota((groups, LANES), 1)
    flags = jnp.where(lane == cap, count, flags)
    out_ref[...] = jnp.where(lane == cap + 1, length.astype(jnp.float32), flags)


def stats_kernel(
    objectives, hidden_ref, weight_ref, text_ref, gain_ref, head_ref, visual_ref, stats_ref, total, stats
):
    step = pl.program_id(0)
    tokens = total.shape[0]
    gained = jnp.concatenate(in_three(gain_ref[...] * head_ref[...]), axis=0)

    def of_rows(x):
        parts = dot32(gained, x, LAST)
        value = parts[:K_ROWS] + parts[K_ROWS : 2 * K_ROWS] + parts[2 * K_ROWS :]
        wide = x.astype(jnp.float32)
        square = wide * wide
        high = square.astype(jnp.bfloat16)
        low = (square - high.astype(jnp.float32)).astype(jnp.bfloat16)
        ones = jnp.ones((K_ROWS, x.shape[1]), jnp.bfloat16)
        squares = dot32(ones, high, LAST) + dot32(ones, low, LAST)
        return jnp.where(iota(value.shape, 0) == objectives, squares, value)

    part = dot32(hidden_ref[...], weight_ref[...], (((1,), (0,)), ((), ())))

    @pl.when(step == 0)
    def _():
        total[...] = part

    @pl.when(step > 0)
    def _():
        total[...] += part

    rows = text_ref.shape[0]
    stats[:, pl.ds(pl.multiple_of(tokens + step * rows, LANES), rows)] = of_rows(text_ref[...])

    @pl.when(step == pl.num_programs(0) - 1)
    def _():
        visual = total[...].astype(jnp.bfloat16)
        visual_ref[...] = visual
        stats[:, :tokens] = of_rows(visual)
        for copy in range(stats_ref.shape[0]):
            stats_ref[copy] = stats[...]


def pooled_kernel(
    cap,
    objectives,
    features,
    me_ref,
    length_ref,
    stats_ref,
    flags_ref,
    owner_ref,
    rows_ref,
    targets_ref,
    visual_ref,
    text_ref,
    pooled_ref,
    kept_ref,
):
    tokens, width = visual_ref.shape
    positions = text_ref.shape[0]
    groups = flags_ref.shape[0]
    slots = rows_ref.shape[1]
    stats = stats_ref[0]
    for part in range(1, stats_ref.shape[0]):
        stats = stats + stats_ref[part]
    inv = lax.rsqrt(stats[objectives : objectives + 1] / features + EPSILON)
    flags = flags_ref[...]

    owned = owner_ref[...] == iota((groups, tokens), 0)
    member = owned.astype(jnp.bfloat16)
    before = (iota((tokens, tokens), 0) < iota((tokens, tokens), 1)).astype(jnp.bfloat16)
    earlier = dot32(member, before, (((1,), (0,)), ((), ())))
    rank = jnp.sum(jnp.where(owned, earlier, 0.0), axis=0, keepdims=True)
    told = dot_exact(flags, owned.astype(jnp.float32), FIRST)
    at = iota(told.shape, 0)
    live = jnp.sum(
        jnp.where((at < cap) & (at == rank.astype(jnp.int32)), told, 0.0), axis=0, keepdims=True
    )
    token_inv = inv[:, :tokens]
    token_weight = live * token_inv / told[cap + 1 : cap + 2]

    length = length_ref[0]
    slot = iota((groups, slots), 1)
    first = iota((groups, slots), 0) * cap
    count = flags[:, cap : cap + 1].astype(jnp.int32)
    used = jnp.sum(((slot >= first) & (slot < first + count)).astype(jnp.float32), axis=0, keepdims=True)
    row = rows_ref[...]
    tall = positions // LANES
    high = jnp.where(lax.div(row, LANES) == iota((tall, slots), 0), used, 0.0).astype(jnp.bfloat16)
    low = (lax.rem(row, LANES) == iota((LANES, slots), 0)).astype(jnp.bfloat16)
    replaced = dot32(high, low, LAST)
    replaced = jnp.concatenate([replaced[i : i + 1] for i in range(tall)], axis=1)
    stays = (iota((1, positions), 1) < length) & (replaced < 0.5)
    text_weight = jnp.where(stays, inv[:, tokens:], 0.0) / length.astype(jnp.float32)

    along = (((1,), (0,)), ((), ()))
    spread = jnp.where(owned, token_weight, 0.0)
    three = dot32(jnp.concatenate(in_three(spread), axis=0), visual_ref[...], along)
    pooled = three[:groups] + three[groups : 2 * groups] + three[2 * groups :]
    reward = dot_exact(spread, stats[:, :tokens], LAST)
    split = jnp.concatenate(in_three(jnp.broadcast_to(text_weight, (16, positions))), axis=0)
    text_three = dot32(split, text_ref[...], along)
    text_pooled = text_three[0:1] + text_three[16:17] + text_three[32:33]
    text_reward = dot_exact(
        jnp.broadcast_to(text_weight, (8, positions)), stats[:, tokens:], LAST
    )[0:1]
    mine = iota((groups, 1), 0) == me_ref[0]
    pooled_ref[:, :width] = pooled + jnp.where(mine, text_pooled, 0.0)
    reward = reward + jnp.where(mine, text_reward, 0.0)
    target = jnp.where(mine, targets_ref[...], 0.0)
    pooled_ref[:, width:] = jnp.zeros((groups, LANES), jnp.float32)
    pooled_ref[:, width : width + objectives] = reward[:, :objectives]
    pooled_ref[:, width + TARGET_AT : width + TARGET_AT + objectives] = target
    kept = jnp.where(iota((K_ROWS, tokens), 0) == objectives, token_weight, stats[:, :tokens])
    factor = token_weight * token_inv * token_inv / features
    kept_ref[...] = jnp.where(iota((K_ROWS, tokens), 0) == objectives + 1, factor, kept)


def grads_kernel(
    objectives,
    scale,
    me_ref,
    pooled_ref,
    kept_ref,
    owner_ref,
    visual_ref,
    labels_ref,
    gain_ref,
    head_ref,
    reward_ref,
    visual_grad_ref,
    head_grad_ref,
    gain_grad_ref,
):
    tokens, width = visual_ref.shape
    groups = pooled_ref.shape[0]
    z = pooled_ref[:, :width]
    rest = pooled_ref[:, width:]
    mine = iota(rest.shape, 0) == me_ref[0]
    reward_ref[...] = jnp.sum(jnp.where(mine, rest, 0.0), axis=0, keepdims=True)
    turned = rest.T
    labels = labels_ref[...].astype(jnp.float32)
    count = jnp.maximum(jnp.sum(labels, axis=1, keepdims=True), 1.0)
    error = turned[:K_ROWS] - turned[TARGET_AT : TARGET_AT + K_ROWS]
    cot = scale * labels * error / count
    gain = gain_ref[...]
    head = head_ref[...]
    along = (((1,), (0,)), ((), ()))
    head_grad_ref[...] = (gain * dot_exact(cot, z, along))[:objectives]
    direction = dot_exact(cot, head, FIRST)
    gain_grad_ref[...] = jnp.sum(z * direction, axis=0, keepdims=True)
    owned = owner_ref[...] == iota((groups, tokens), 0)
    kept = kept_ref[...]
    own_cot = dot_exact(cot, owned.astype(jnp.float32), along)
    is_value = iota(kept.shape, 0) < objectives
    row_dot = jnp.sum(jnp.where(is_value, kept * own_cot, 0.0), axis=0, keepdims=True)
    weight = kept[objectives : objectives + 1]
    beta = kept[objectives + 1 : objectives + 2] * row_dot
    both = jnp.concatenate([weight, beta, jnp.zeros((LANES - 2, tokens), jnp.float32)], axis=0)
    columns = both.T
    member = owned.astype(jnp.bfloat16)
    directions = jnp.concatenate(in_three(gain * direction), axis=0)
    own = dot32(jnp.concatenate([member] * 3, axis=0), directions, FIRST)
    grad = columns[:, 0:1] * own - columns[:, 1:2] * visual_ref[...].astype(jnp.float32)
    visual_grad_ref[...] = grad.astype(jnp.bfloat16)


def whole(count):
    return [pl.BlockSpec(memory_space=pltpu.VMEM)] * count


def scalars(count):
    return [pl.BlockSpec(memory_space=pltpu.SMEM)] * count


def to_all(array, axis):
    copies = jnp.broadcast_to(array, (lax.axis_size(axis), *array.shape))
    return lax.all_to_all(copies, axis, split_axis=0, concat_axis=0, tiled=True)


def on_device(
    hidden, merge_weight, text_embed, gain, head_weight, owner, vis_row, lengths, labels, targets
):
    groups, near = lax.axis_size(GRP), lax.axis_size(NEAR)
    tokens, depth = hidden.shape
    positions, width = text_embed.shape
    objectives = head_weight.shape[1]
    cap = vis_row.shape[1] // groups
    features = float(width * lax.axis_size(TP))
    scale = float(positions * groups // 16)
    me = lax.axis_index(GRP).astype(jnp.int32).reshape(1)
    owners = owner.reshape(1, tokens)
    gain_row = gain.reshape(1, width)
    head = jnp.pad(head_weight.T, ((0, K_ROWS - objectives), (0, 0)))
    marks = jnp.pad(labels.T, ((0, K_ROWS - objectives), (0, 0)))

    flags = pl.pallas_call(
        functools.partial(flags_kernel, cap),
        out_shape=jax.ShapeDtypeStruct((groups, LANES), jnp.float32),
        in_specs=scalars(1) + whole(2),
        out_specs=pl.BlockSpec(memory_space=pltpu.VMEM),
        compiler_params=VMEM,
        name="flags",
    )(lengths, owners, vis_row)
    told = lax.all_to_all(
        flags.reshape(groups, 1, LANES), GRP, split_axis=0, concat_axis=0, tiled=True
    ).reshape(groups, LANES)

    steps = 8
    rows = tokens + positions
    copies = lax.axis_size("tx")
    visual, stats = pl.pallas_call(
        functools.partial(stats_kernel, objectives),
        grid=(steps,),
        out_shape=(
            jax.ShapeDtypeStruct((tokens, width), jnp.bfloat16),
            jax.ShapeDtypeStruct((copies, K_ROWS, rows), jnp.float32),
        ),
        in_specs=[
            pl.BlockSpec((tokens, depth // steps), lambda i: (0, i)),
            pl.BlockSpec((depth // steps, width), lambda i: (i, 0)),
            pl.BlockSpec((positions // steps, width), lambda i: (i, 0)),
            pl.BlockSpec((1, width), lambda i: (0, 0)),
            pl.BlockSpec((K_ROWS, width), lambda i: (0, 0)),
        ],
        out_specs=(
            pl.BlockSpec((tokens, width), lambda i: (0, 0)),
            pl.BlockSpec((copies, K_ROWS, rows), lambda i: (0, 0, 0)),
        ),
        scratch_shapes=[
            pltpu.VMEM((tokens, width), jnp.float32),
            pltpu.VMEM((K_ROWS, rows), jnp.float32),
        ],
        compiler_params=VMEM,
        name="stats",
    )(hidden, merge_weight, text_embed, gain_row, head)
    stats = lax.all_to_all(stats, "tx", split_axis=0, concat_axis=0, tiled=True)
    stats = to_all(jnp.sum(stats, axis=0), "ty")

    pooled, kept = pl.pallas_call(
        functools.partial(pooled_kernel, cap, objectives, features),
        out_shape=(
            jax.ShapeDtypeStruct((groups, width + LANES), jnp.float32),
            jax.ShapeDtypeStruct((K_ROWS, tokens), jnp.float32),
        ),
        in_specs=scalars(2) + whole(7),
        out_specs=tuple(whole(2)),
        compiler_params=VMEM,
        name="pooled",
    )(me, lengths, stats, told, owners, vis_row, targets, visual, text_embed)
    block = pooled.reshape(near, groups // near, width + LANES)
    block = jnp.sum(lax.all_to_all(block, NEAR, split_axis=0, concat_axis=0, tiled=True), axis=0)
    block = jnp.sum(to_all(block, "far"), axis=0)
    pooled = to_all(block, NEAR).reshape(groups, width + LANES)

    reward, visual_grad, head_grad, gain_grad = pl.pallas_call(
        functools.partial(grads_kernel, objectives, scale),
        out_shape=(
            jax.ShapeDtypeStruct((1, LANES), jnp.float32),
            jax.ShapeDtypeStruct((tokens, width), jnp.bfloat16),
            jax.ShapeDtypeStruct((objectives, width), jnp.float32),
            jax.ShapeDtypeStruct((1, width), jnp.float32),
        ),
        in_specs=scalars(1) + whole(7),
        out_specs=tuple(whole(4)),
        compiler_params=VMEM,
        name="grads",
    )(me, pooled, kept, owners, visual, marks, gain_row, head)
    return reward[:, :objectives], visual_grad, head_grad.T, gain_grad.reshape(width)


def solution(mesh):
    groups, tp = mesh.shape["grp"], mesh.shape["tp"]
    near = 4 if groups % 16 == 0 else 2
    ty = 4 if tp % 16 == 0 else 1
    torus = Mesh(
        mesh.devices.reshape(groups // (2 * near), near, 2, ty, tp // ty),
        ("far", "near", "core", "ty", "tx"),
    )
    placed = (
        P(GRP, None),
        P(None, TP),
        P(GRP, TP),
        P(TP),
        P(TP, None),
        P(GRP, None),
        P(GRP, None),
        P(GRP),
        P(),
        P(GRP, None),
    )
    return jax.shard_map(
        on_device,
        mesh=torus,
        in_specs=placed,
        out_specs=(P(GRP, None), P(GRP, TP), P(TP, None), P(TP)),
        check_vma=False,
    )
```

```python
import functools

import jax
import jax.numpy as jnp
from jax import lax
from jax.experimental import pallas as pl
from jax.experimental.pallas import tpu as pltpu
from jax.sharding import Mesh
from jax.sharding import PartitionSpec as P

GRP = ("far", "near", "core")
NEAR = ("near", "core")
TP = ("ty", "tx")
EPSILON = 1e-06
LANES = 128
K_ROWS = 24
TARGET_AT = 32
VMEM = pltpu.CompilerParams(vmem_limit_bytes=48 * 2**20)
EXACT = lax.Precision.HIGHEST
LAST = (((1,), (1,)), ((), ()))
FIRST = (((0,), (0,)), ((), ()))


def iota(shape, dim):
    return lax.broadcasted_iota(jnp.int32, shape, dim)


def in_three(x):
    hi = x.astype(jnp.bfloat16)
    rest = x - hi.astype(jnp.float32)
    mid = rest.astype(jnp.bfloat16)
    return hi, mid, (rest - mid.astype(jnp.float32)).astype(jnp.bfloat16)


def dot32(a, b, dims):
    return lax.dot_general(a, b, dims, preferred_element_type=jnp.float32)


def dot_exact(a, b, dims):
    return lax.dot_general(a, b, dims, precision=EXACT, preferred_element_type=jnp.float32)


def flags_kernel(cap, length_ref, owner_ref, rows_ref, out_ref):
    groups = out_ref.shape[0]
    slots = rows_ref.shape[1]
    length = length_ref[0]
    live = (rows_ref[...] < length).astype(jnp.float32)
    slot = iota((groups, slots), 1)
    first = iota((groups, slots), 0) * cap
    mine = jnp.where((slot >= first) & (slot < first + cap), live, 0.0).astype(jnp.bfloat16)
    rank = lax.rem(iota((LANES, slots), 1), cap)
    place = (rank == iota((LANES, slots), 0)).astype(jnp.bfloat16)
    flags = dot32(mine, place, LAST)
    owned = (owner_ref[...] == iota((groups, owner_ref.shape[1]), 0)).astype(jnp.float32)
    count = jnp.sum(owned, axis=1, keepdims=True)
    lane = iota((groups, LANES), 1)
    flags = jnp.where(lane == cap, count, flags)
    out_ref[...] = jnp.where(lane == cap + 1, length.astype(jnp.float32), flags)


def stats_kernel(
    objectives,
    after_ref,
    hidden_ref,
    weight_ref,
    text_ref,
    gain_ref,
    head_ref,
    visual_ref,
    stats_ref,
    total,
    stats,
):
    step = pl.program_id(0)
    tokens = total.shape[0]
    gained = jnp.concatenate(in_three(gain_ref[...] * head_ref[...]), axis=0)

    def of_rows(x):
        parts = dot32(gained, x, LAST)
        value = parts[:K_ROWS] + parts[K_ROWS : 2 * K_ROWS] + parts[2 * K_ROWS :]
        wide = x.astype(jnp.float32)
        square = wide * wide
        high = square.astype(jnp.bfloat16)
        low = (square - high.astype(jnp.float32)).astype(jnp.bfloat16)
        ones = jnp.ones((K_ROWS, x.shape[1]), jnp.bfloat16)
        squares = dot32(ones, high, LAST) + dot32(ones, low, LAST)
        return jnp.where(iota(value.shape, 0) == objectives, squares, value)

    part = dot32(hidden_ref[...], weight_ref[...], (((1,), (0,)), ((), ())))

    @pl.when(step == 0)
    def _():
        total[...] = part

    @pl.when(step > 0)
    def _():
        total[...] += part

    rows = text_ref.shape[0]
    stats[:, pl.ds(pl.multiple_of(tokens + step * rows, LANES), rows)] = of_rows(text_ref[...])

    @pl.when(step == pl.num_programs(0) - 1)
    def _():
        visual = total[...].astype(jnp.bfloat16)
        visual_ref[...] = visual
        stats[:, :tokens] = of_rows(visual)
        for copy in range(stats_ref.shape[0]):
            stats_ref[copy] = stats[...]


def pooled_kernel(
    cap,
    objectives,
    features,
    me_ref,
    length_ref,
    stats_ref,
    flags_ref,
    owner_ref,
    rows_ref,
    targets_ref,
    visual_ref,
    text_ref,
    pooled_ref,
    kept_ref,
):
    tokens, width = visual_ref.shape
    positions = text_ref.shape[0]
    groups = flags_ref.shape[0]
    slots = rows_ref.shape[1]
    stats = stats_ref[0]
    for part in range(1, stats_ref.shape[0]):
        stats = stats + stats_ref[part]
    inv = lax.rsqrt(stats[objectives : objectives + 1] / features + EPSILON)
    flags = flags_ref[...]

    owned = owner_ref[...] == iota((groups, tokens), 0)
    member = owned.astype(jnp.bfloat16)
    before = (iota((tokens, tokens), 0) < iota((tokens, tokens), 1)).astype(jnp.bfloat16)
    earlier = dot32(member, before, (((1,), (0,)), ((), ())))
    rank = jnp.sum(jnp.where(owned, earlier, 0.0), axis=0, keepdims=True)
    told = dot_exact(flags, owned.astype(jnp.float32), FIRST)
    at = iota(told.shape, 0)
    live = jnp.sum(
        jnp.where((at < cap) & (at == rank.astype(jnp.int32)), told, 0.0), axis=0, keepdims=True
    )
    token_inv = inv[:, :tokens]
    token_weight = live * token_inv / told[cap + 1 : cap + 2]

    length = length_ref[0]
    slot = iota((groups, slots), 1)
    first = iota((groups, slots), 0) * cap
    count = flags[:, cap : cap + 1].astype(jnp.int32)
    used = jnp.sum(((slot >= first) & (slot < first + count)).astype(jnp.float32), axis=0, keepdims=True)
    row = rows_ref[...]
    tall = positions // LANES
    high = jnp.where(lax.div(row, LANES) == iota((tall, slots), 0), used, 0.0).astype(jnp.bfloat16)
    low = (lax.rem(row, LANES) == iota((LANES, slots), 0)).astype(jnp.bfloat16)
    replaced = dot32(high, low, LAST)
    replaced = jnp.concatenate([replaced[i : i + 1] for i in range(tall)], axis=1)
    stays = (iota((1, positions), 1) < length) & (replaced < 0.5)
    text_weight = jnp.where(stays, inv[:, tokens:], 0.0) / length.astype(jnp.float32)

    along = (((1,), (0,)), ((), ()))
    spread = jnp.where(owned, token_weight, 0.0)
    three = dot32(jnp.concatenate(in_three(spread), axis=0), visual_ref[...], along)
    pooled = three[:groups] + three[groups : 2 * groups] + three[2 * groups :]
    reward = dot_exact(spread, stats[:, :tokens], LAST)
    split = jnp.concatenate(in_three(jnp.broadcast_to(text_weight, (16, positions))), axis=0)
    text_three = dot32(split, text_ref[...], along)
    text_pooled = text_three[0:1] + text_three[16:17] + text_three[32:33]
    text_reward = dot_exact(
        jnp.broadcast_to(text_weight, (8, positions)), stats[:, tokens:], LAST
    )[0:1]
    mine = iota((groups, 1), 0) == me_ref[0]
    pooled_ref[:, :width] = pooled + jnp.where(mine, text_pooled, 0.0)
    reward = reward + jnp.where(mine, text_reward, 0.0)
    target = jnp.where(mine, targets_ref[...], 0.0)
    pooled_ref[:, width:] = jnp.zeros((groups, LANES), jnp.float32)
    pooled_ref[:, width : width + objectives] = reward[:, :objectives]
    pooled_ref[:, width + TARGET_AT : width + TARGET_AT + objectives] = target
    kept = jnp.where(iota((K_ROWS, tokens), 0) == objectives, token_weight, stats[:, :tokens])
    factor = token_weight * token_inv * token_inv / features
    kept_ref[...] = jnp.where(iota((K_ROWS, tokens), 0) == objectives + 1, factor, kept)


def grads_kernel(
    objectives,
    scale,
    me_ref,
    pooled_ref,
    kept_ref,
    owner_ref,
    visual_ref,
    labels_ref,
    gain_ref,
    head_ref,
    reward_ref,
    visual_grad_ref,
    head_grad_ref,
    gain_grad_ref,
):
    tokens, width = visual_ref.shape
    groups = pooled_ref.shape[0]
    z = pooled_ref[:, :width]
    rest = pooled_ref[:, width:]
    mine = iota(rest.shape, 0) == me_ref[0]
    reward_ref[...] = jnp.sum(jnp.where(mine, rest, 0.0), axis=0, keepdims=True)
    turned = rest.T
    labels = labels_ref[...].astype(jnp.float32)
    count = jnp.maximum(jnp.sum(labels, axis=1, keepdims=True), 1.0)
    error = turned[:K_ROWS] - turned[TARGET_AT : TARGET_AT + K_ROWS]
    cot = scale * labels * error / count
    gain = gain_ref[...]
    head = head_ref[...]
    along = (((1,), (0,)), ((), ()))
    head_grad_ref[...] = (gain * dot_exact(cot, z, along))[:objectives]
    direction = dot_exact(cot, head, FIRST)
    gain_grad_ref[...] = jnp.sum(z * direction, axis=0, keepdims=True)
    owned = owner_ref[...] == iota((groups, tokens), 0)
    kept = kept_ref[...]
    own_cot = dot_exact(cot, owned.astype(jnp.float32), along)
    is_value = iota(kept.shape, 0) < objectives
    row_dot = jnp.sum(jnp.where(is_value, kept * own_cot, 0.0), axis=0, keepdims=True)
    weight = kept[objectives : objectives + 1]
    beta = kept[objectives + 1 : objectives + 2] * row_dot
    both = jnp.concatenate([weight, beta, jnp.zeros((LANES - 2, tokens), jnp.float32)], axis=0)
    columns = both.T
    member = owned.astype(jnp.bfloat16)
    directions = jnp.concatenate(in_three(gain * direction), axis=0)
    own = dot32(jnp.concatenate([member] * 3, axis=0), directions, FIRST)
    grad = columns[:, 0:1] * own - columns[:, 1:2] * visual_ref[...].astype(jnp.float32)
    visual_grad_ref[...] = grad.astype(jnp.bfloat16)


def whole(count):
    return [pl.BlockSpec(memory_space=pltpu.VMEM)] * count


def scalars(count):
    return [pl.BlockSpec(memory_space=pltpu.SMEM)] * count


def to_all(array, axis):
    copies = jnp.broadcast_to(array, (lax.axis_size(axis), *array.shape))
    return lax.all_to_all(copies, axis, split_axis=0, concat_axis=0, tiled=True)


def on_device(
    hidden, merge_weight, text_embed, gain, head_weight, owner, vis_row, lengths, labels, targets
):
    groups, near = lax.axis_size(GRP), lax.axis_size(NEAR)
    tokens, depth = hidden.shape
    positions, width = text_embed.shape
    objectives = head_weight.shape[1]
    cap = vis_row.shape[1] // groups
    features = float(width * lax.axis_size(TP))
    scale = float(positions * groups // 16)
    me = lax.axis_index(GRP).astype(jnp.int32).reshape(1)
    owners = owner.reshape(1, tokens)
    gain_row = gain.reshape(1, width)
    head = jnp.pad(head_weight.T, ((0, K_ROWS - objectives), (0, 0)))
    marks = jnp.pad(labels.T, ((0, K_ROWS - objectives), (0, 0)))

    flags = pl.pallas_call(
        functools.partial(flags_kernel, cap),
        out_shape=jax.ShapeDtypeStruct((groups, LANES), jnp.float32),
        in_specs=scalars(1) + whole(2),
        out_specs=pl.BlockSpec(memory_space=pltpu.VMEM),
        compiler_params=VMEM,
        name="flags",
    )(lengths, owners, vis_row)
    told = lax.all_to_all(
        flags.reshape(groups, 1, LANES), GRP, split_axis=0, concat_axis=0, tiled=True
    ).reshape(groups, LANES)

    steps = 8
    rows = tokens + positions
    copies = lax.axis_size("tx")
    visual, stats = pl.pallas_call(
        functools.partial(stats_kernel, objectives),
        grid=(steps,),
        out_shape=(
            jax.ShapeDtypeStruct((tokens, width), jnp.bfloat16),
            jax.ShapeDtypeStruct((copies, K_ROWS, rows), jnp.float32),
        ),
        in_specs=[
            pl.BlockSpec(memory_space=pl.ANY),
            pl.BlockSpec((tokens, depth // steps), lambda i: (0, i)),
            pl.BlockSpec((depth // steps, width), lambda i: (i, 0)),
            pl.BlockSpec((positions // steps, width), lambda i: (i, 0)),
            pl.BlockSpec((1, width), lambda i: (0, 0)),
            pl.BlockSpec((K_ROWS, width), lambda i: (0, 0)),
        ],
        out_specs=(
            pl.BlockSpec((tokens, width), lambda i: (0, 0)),
            pl.BlockSpec((copies, K_ROWS, rows), lambda i: (0, 0, 0)),
        ),
        scratch_shapes=[
            pltpu.VMEM((tokens, width), jnp.float32),
            pltpu.VMEM((K_ROWS, rows), jnp.float32),
        ],
        compiler_params=VMEM,
        name="stats",
    )(flags, hidden, merge_weight, text_embed, gain_row, head)
    stats, told = lax.optimization_barrier((stats, told))
    stats = lax.all_to_all(stats, "tx", split_axis=0, concat_axis=0, tiled=True)
    stats = to_all(jnp.sum(stats, axis=0), "ty")

    pooled, kept = pl.pallas_call(
        functools.partial(pooled_kernel, cap, objectives, features),
        out_shape=(
            jax.ShapeDtypeStruct((groups, width + LANES), jnp.float32),
            jax.ShapeDtypeStruct((K_ROWS, tokens), jnp.float32),
        ),
        in_specs=scalars(2) + whole(7),
        out_specs=tuple(whole(2)),
        compiler_params=VMEM,
        name="pooled",
    )(me, lengths, stats, told, owners, vis_row, targets, visual, text_embed)
    block = pooled.reshape(near, groups // near, width + LANES)
    block = jnp.sum(lax.all_to_all(block, NEAR, split_axis=0, concat_axis=0, tiled=True), axis=0)
    block = jnp.sum(to_all(block, "far"), axis=0)
    pooled = to_all(block, NEAR).reshape(groups, width + LANES)

    reward, visual_grad, head_grad, gain_grad = pl.pallas_call(
        functools.partial(grads_kernel, objectives, scale),
        out_shape=(
            jax.ShapeDtypeStruct((1, LANES), jnp.float32),
            jax.ShapeDtypeStruct((tokens, width), jnp.bfloat16),
            jax.ShapeDtypeStruct((objectives, width), jnp.float32),
            jax.ShapeDtypeStruct((1, width), jnp.float32),
        ),
        in_specs=scalars(1) + whole(7),
        out_specs=tuple(whole(4)),
        compiler_params=VMEM,
        name="grads",
    )(me, pooled, kept, owners, visual, marks, gain_row, head)
    return reward[:, :objectives], visual_grad, head_grad.T, gain_grad.reshape(width)


def solution(mesh):
    groups, tp = mesh.shape["grp"], mesh.shape["tp"]
    near = 8 if groups % 32 == 0 else 2
    ty = 4 if tp % 16 == 0 else 1
    torus = Mesh(
        mesh.devices.reshape(groups // (2 * near), near, 2, ty, tp // ty),
        ("far", "near", "core", "ty", "tx"),
    )
    placed = (
        P(GRP, None),
        P(None, TP),
        P(GRP, TP),
        P(TP),
        P(TP, None),
        P(GRP, None),
        P(GRP, None),
        P(GRP),
        P(),
        P(GRP, None),
    )
    return jax.shard_map(
        on_device,
        mesh=torus,
        in_specs=placed,
        out_specs=(P(GRP, None), P(GRP, TP), P(TP, None), P(TP)),
        check_vma=False,
    )
```

```python
import functools

import jax
import jax.numpy as jnp
from jax import lax
from jax.experimental import pallas as pl
from jax.experimental.pallas import tpu as pltpu
from jax.sharding import Mesh
from jax.sharding import PartitionSpec as P

GRP = ("far", "near", "core")
NEAR = ("near", "core")
TP = ("ty", "tx")
EPSILON = 1e-06
LANES = 128
K_ROWS = 24
TARGET_AT = 32
VMEM = pltpu.CompilerParams(vmem_limit_bytes=48 * 2**20)
EXACT = lax.Precision.HIGHEST
LAST = (((1,), (1,)), ((), ()))
FIRST = (((0,), (0,)), ((), ()))


def iota(shape, dim):
    return lax.broadcasted_iota(jnp.int32, shape, dim)


def in_three(x):
    hi = x.astype(jnp.bfloat16)
    rest = x - hi.astype(jnp.float32)
    mid = rest.astype(jnp.bfloat16)
    return hi, mid, (rest - mid.astype(jnp.float32)).astype(jnp.bfloat16)


def dot32(a, b, dims):
    return lax.dot_general(a, b, dims, preferred_element_type=jnp.float32)


def dot_exact(a, b, dims):
    return lax.dot_general(a, b, dims, precision=EXACT, preferred_element_type=jnp.float32)


def flags_kernel(cap, length_ref, owner_ref, rows_ref, out_ref):
    groups = out_ref.shape[0]
    slots = rows_ref.shape[1]
    length = length_ref[0]
    live = (rows_ref[...] < length).astype(jnp.float32)
    slot = iota((groups, slots), 1)
    first = iota((groups, slots), 0) * cap
    mine = jnp.where((slot >= first) & (slot < first + cap), live, 0.0).astype(jnp.bfloat16)
    rank = lax.rem(iota((LANES, slots), 1), cap)
    place = (rank == iota((LANES, slots), 0)).astype(jnp.bfloat16)
    flags = dot32(mine, place, LAST)
    owned = (owner_ref[...] == iota((groups, owner_ref.shape[1]), 0)).astype(jnp.float32)
    count = jnp.sum(owned, axis=1, keepdims=True)
    lane = iota((groups, LANES), 1)
    flags = jnp.where(lane == cap, count, flags)
    out_ref[...] = jnp.where(lane == cap + 1, length.astype(jnp.float32), flags)


def stats_kernel(
    objectives,
    after_ref,
    hidden_ref,
    weight_ref,
    text_ref,
    gain_ref,
    head_ref,
    visual_ref,
    stats_ref,
    total,
    stats,
):
    step = pl.program_id(0)
    tokens = total.shape[0]
    gained = jnp.concatenate(in_three(gain_ref[...] * head_ref[...]), axis=0)

    def of_rows(x):
        parts = dot32(gained, x, LAST)
        value = parts[:K_ROWS] + parts[K_ROWS : 2 * K_ROWS] + parts[2 * K_ROWS :]
        wide = x.astype(jnp.float32)
        square = wide * wide
        high = square.astype(jnp.bfloat16)
        low = (square - high.astype(jnp.float32)).astype(jnp.bfloat16)
        ones = jnp.ones((K_ROWS, x.shape[1]), jnp.bfloat16)
        squares = dot32(ones, high, LAST) + dot32(ones, low, LAST)
        return jnp.where(iota(value.shape, 0) == objectives, squares, value)

    part = dot32(hidden_ref[...], weight_ref[...], (((1,), (0,)), ((), ())))

    @pl.when(step == 0)
    def _():
        total[...] = part

    @pl.when(step > 0)
    def _():
        total[...] += part

    rows = text_ref.shape[0]
    stats[:, pl.ds(pl.multiple_of(tokens + step * rows, LANES), rows)] = of_rows(text_ref[...])

    @pl.when(step == pl.num_programs(0) - 1)
    def _():
        visual = total[...].astype(jnp.bfloat16)
        visual_ref[...] = visual
        stats[:, :tokens] = of_rows(visual)
        stats_ref[...] = stats[...]


def pooled_kernel(
    cap,
    objectives,
    features,
    me_ref,
    length_ref,
    stats_ref,
    flags_ref,
    owner_ref,
    rows_ref,
    targets_ref,
    visual_ref,
    text_ref,
    pooled_ref,
    kept_ref,
):
    tokens, width = visual_ref.shape
    positions = text_ref.shape[0]
    groups = flags_ref.shape[0]
    slots = rows_ref.shape[1]
    stats = stats_ref[0]
    for part in range(1, stats_ref.shape[0]):
        stats = stats + stats_ref[part]
    inv = lax.rsqrt(stats[objectives : objectives + 1] / features + EPSILON)
    flags = flags_ref[...]

    owned = owner_ref[...] == iota((groups, tokens), 0)
    member = owned.astype(jnp.bfloat16)
    before = (iota((tokens, tokens), 0) < iota((tokens, tokens), 1)).astype(jnp.bfloat16)
    earlier = dot32(member, before, (((1,), (0,)), ((), ())))
    rank = jnp.sum(jnp.where(owned, earlier, 0.0), axis=0, keepdims=True)
    told = dot_exact(flags, owned.astype(jnp.float32), FIRST)
    at = iota(told.shape, 0)
    live = jnp.sum(
        jnp.where((at < cap) & (at == rank.astype(jnp.int32)), told, 0.0), axis=0, keepdims=True
    )
    token_inv = inv[:, :tokens]
    token_weight = live * token_inv / told[cap + 1 : cap + 2]

    length = length_ref[0]
    slot = iota((groups, slots), 1)
    first = iota((groups, slots), 0) * cap
    count = flags[:, cap : cap + 1].astype(jnp.int32)
    used = jnp.sum(((slot >= first) & (slot < first + count)).astype(jnp.float32), axis=0, keepdims=True)
    row = rows_ref[...]
    tall = positions // LANES
    high = jnp.where(lax.div(row, LANES) == iota((tall, slots), 0), used, 0.0).astype(jnp.bfloat16)
    low = (lax.rem(row, LANES) == iota((LANES, slots), 0)).astype(jnp.bfloat16)
    replaced = dot32(high, low, LAST)
    replaced = jnp.concatenate([replaced[i : i + 1] for i in range(tall)], axis=1)
    stays = (iota((1, positions), 1) < length) & (replaced < 0.5)
    text_weight = jnp.where(stays, inv[:, tokens:], 0.0) / length.astype(jnp.float32)

    along = (((1,), (0,)), ((), ()))
    spread = jnp.where(owned, token_weight, 0.0)
    three = dot32(jnp.concatenate(in_three(spread), axis=0), visual_ref[...], along)
    pooled = three[:groups] + three[groups : 2 * groups] + three[2 * groups :]
    reward = dot_exact(spread, stats[:, :tokens], LAST)
    split = jnp.concatenate(in_three(jnp.broadcast_to(text_weight, (16, positions))), axis=0)
    text_three = dot32(split, text_ref[...], along)
    text_pooled = text_three[0:1] + text_three[16:17] + text_three[32:33]
    text_reward = dot_exact(
        jnp.broadcast_to(text_weight, (8, positions)), stats[:, tokens:], LAST
    )[0:1]
    mine = iota((groups, 1), 0) == me_ref[0]
    pooled_ref[:, :width] = pooled + jnp.where(mine, text_pooled, 0.0)
    reward = reward + jnp.where(mine, text_reward, 0.0)
    target = jnp.where(mine, targets_ref[...], 0.0)
    pooled_ref[:, width:] = jnp.zeros((groups, LANES), jnp.float32)
    pooled_ref[:, width : width + objectives] = reward[:, :objectives]
    pooled_ref[:, width + TARGET_AT : width + TARGET_AT + objectives] = target
    kept = jnp.where(iota((K_ROWS, tokens), 0) == objectives, token_weight, stats[:, :tokens])
    factor = token_weight * token_inv * token_inv / features
    kept_ref[...] = jnp.where(iota((K_ROWS, tokens), 0) == objectives + 1, factor, kept)


def grads_kernel(
    objectives,
    scale,
    me_ref,
    pooled_ref,
    kept_ref,
    owner_ref,
    visual_ref,
    labels_ref,
    gain_ref,
    head_ref,
    reward_ref,
    visual_grad_ref,
    head_grad_ref,
    gain_grad_ref,
):
    tokens, width = visual_ref.shape
    groups = pooled_ref.shape[0]
    z = pooled_ref[:, :width]
    rest = pooled_ref[:, width:]
    mine = iota(rest.shape, 0) == me_ref[0]
    reward_ref[...] = jnp.sum(jnp.where(mine, rest, 0.0), axis=0, keepdims=True)
    turned = rest.T
    labels = labels_ref[...].astype(jnp.float32)
    count = jnp.maximum(jnp.sum(labels, axis=1, keepdims=True), 1.0)
    error = turned[:K_ROWS] - turned[TARGET_AT : TARGET_AT + K_ROWS]
    cot = scale * labels * error / count
    gain = gain_ref[...]
    head = head_ref[...]
    along = (((1,), (0,)), ((), ()))
    head_grad_ref[...] = (gain * dot_exact(cot, z, along))[:objectives]
    direction = dot_exact(cot, head, FIRST)
    gain_grad_ref[...] = jnp.sum(z * direction, axis=0, keepdims=True)
    owned = owner_ref[...] == iota((groups, tokens), 0)
    kept = kept_ref[...]
    own_cot = dot_exact(cot, owned.astype(jnp.float32), along)
    is_value = iota(kept.shape, 0) < objectives
    row_dot = jnp.sum(jnp.where(is_value, kept * own_cot, 0.0), axis=0, keepdims=True)
    weight = kept[objectives : objectives + 1]
    beta = kept[objectives + 1 : objectives + 2] * row_dot
    both = jnp.concatenate([weight, beta, jnp.zeros((LANES - 2, tokens), jnp.float32)], axis=0)
    columns = both.T
    member = owned.astype(jnp.bfloat16)
    directions = jnp.concatenate(in_three(gain * direction), axis=0)
    own = dot32(jnp.concatenate([member] * 3, axis=0), directions, FIRST)
    grad = columns[:, 0:1] * own - columns[:, 1:2] * visual_ref[...].astype(jnp.float32)
    visual_grad_ref[...] = grad.astype(jnp.bfloat16)


def whole(count):
    return [pl.BlockSpec(memory_space=pltpu.VMEM)] * count


def scalars(count):
    return [pl.BlockSpec(memory_space=pltpu.SMEM)] * count


def on_device(
    hidden, merge_weight, text_embed, gain, head_weight, owner, vis_row, lengths, labels, targets
):
    groups, near = lax.axis_size(GRP), lax.axis_size(NEAR)
    tokens, depth = hidden.shape
    positions, width = text_embed.shape
    objectives = head_weight.shape[1]
    cap = vis_row.shape[1] // groups
    features = float(width * lax.axis_size(TP))
    scale = float(positions * groups // 16)
    me = lax.axis_index(GRP).astype(jnp.int32).reshape(1)
    owners = owner.reshape(1, tokens)
    gain_row = gain.reshape(1, width)
    head = jnp.pad(head_weight.T, ((0, K_ROWS - objectives), (0, 0)))
    marks = jnp.pad(labels.T, ((0, K_ROWS - objectives), (0, 0)))

    flags = pl.pallas_call(
        functools.partial(flags_kernel, cap),
        out_shape=jax.ShapeDtypeStruct((groups, LANES), jnp.float32),
        in_specs=scalars(1) + whole(2),
        out_specs=pl.BlockSpec(memory_space=pltpu.VMEM),
        compiler_params=VMEM,
        name="flags",
    )(lengths, owners, vis_row)
    told = lax.all_to_all(
        flags.reshape(groups, 1, LANES), GRP, split_axis=0, concat_axis=0, tiled=True
    ).reshape(groups, LANES)

    steps = 8
    rows = tokens + positions
    visual, stats = pl.pallas_call(
        functools.partial(stats_kernel, objectives),
        grid=(steps,),
        out_shape=(
            jax.ShapeDtypeStruct((tokens, width), jnp.bfloat16),
            jax.ShapeDtypeStruct((K_ROWS, rows), jnp.float32),
        ),
        in_specs=[
            pl.BlockSpec(memory_space=pl.ANY),
            pl.BlockSpec((tokens, depth // steps), lambda i: (0, i)),
            pl.BlockSpec((depth // steps, width), lambda i: (i, 0)),
            pl.BlockSpec((positions // steps, width), lambda i: (i, 0)),
            pl.BlockSpec((1, width), lambda i: (0, 0)),
            pl.BlockSpec((K_ROWS, width), lambda i: (0, 0)),
        ],
        out_specs=(
            pl.BlockSpec((tokens, width), lambda i: (0, 0)),
            pl.BlockSpec((K_ROWS, rows), lambda i: (0, 0)),
        ),
        scratch_shapes=[
            pltpu.VMEM((tokens, width), jnp.float32),
            pltpu.VMEM((K_ROWS, rows), jnp.float32),
        ],
        compiler_params=VMEM,
        name="stats",
    )(flags, hidden, merge_weight, text_embed, gain_row, head)
    stats = lax.all_gather(jnp.sum(lax.all_gather(stats, "tx"), axis=0), "ty")

    pooled, kept = pl.pallas_call(
        functools.partial(pooled_kernel, cap, objectives, features),
        out_shape=(
            jax.ShapeDtypeStruct((groups, width + LANES), jnp.float32),
            jax.ShapeDtypeStruct((K_ROWS, tokens), jnp.float32),
        ),
        in_specs=scalars(2) + whole(7),
        out_specs=tuple(whole(2)),
        compiler_params=VMEM,
        name="pooled",
    )(me, lengths, stats, told, owners, vis_row, targets, visual, text_embed)
    block = pooled.reshape(near, groups // near, width + LANES)
    block = jnp.sum(lax.all_to_all(block, NEAR, split_axis=0, concat_axis=0, tiled=True), axis=0)
    block = jnp.sum(lax.all_gather(block, "far"), axis=0)
    pooled = lax.all_gather(block, NEAR, tiled=True)

    reward, visual_grad, head_grad, gain_grad = pl.pallas_call(
        functools.partial(grads_kernel, objectives, scale),
        out_shape=(
            jax.ShapeDtypeStruct((1, LANES), jnp.float32),
            jax.ShapeDtypeStruct((tokens, width), jnp.bfloat16),
            jax.ShapeDtypeStruct((objectives, width), jnp.float32),
            jax.ShapeDtypeStruct((1, width), jnp.float32),
        ),
        in_specs=scalars(1) + whole(7),
        out_specs=tuple(whole(4)),
        compiler_params=VMEM,
        name="grads",
    )(me, pooled, kept, owners, visual, marks, gain_row, head)
    return reward[:, :objectives], visual_grad, head_grad.T, gain_grad.reshape(width)


def solution(mesh):
    groups, tp = mesh.shape["grp"], mesh.shape["tp"]
    near = 4 if groups % 16 == 0 else 2
    ty = 4 if tp % 16 == 0 else 1
    torus = Mesh(
        mesh.devices.reshape(groups // (2 * near), near, 2, ty, tp // ty),
        ("far", "near", "core", "ty", "tx"),
    )
    placed = (
        P(GRP, None),
        P(None, TP),
        P(GRP, TP),
        P(TP),
        P(TP, None),
        P(GRP, None),
        P(GRP, None),
        P(GRP),
        P(),
        P(GRP, None),
    )
    return jax.shard_map(
        on_device,
        mesh=torus,
        in_specs=placed,
        out_specs=(P(GRP, None), P(GRP, TP), P(TP, None), P(TP)),
        check_vma=False,
    )
```

```python
import functools

import jax
import jax.numpy as jnp
from jax import lax
from jax.experimental import pallas as pl
from jax.experimental.pallas import tpu as pltpu
from jax.sharding import Mesh
from jax.sharding import PartitionSpec as P

GRP = ("far", "near", "core")
NEAR = ("near", "core")
TP = ("ty", "tx")
EPSILON = 1e-06
LANES = 128
K_ROWS = 24
SIDE = 32
VMEM = pltpu.CompilerParams(vmem_limit_bytes=48 * 2**20)
EXACT = lax.Precision.HIGHEST
LAST = (((1,), (1,)), ((), ()))
FIRST = (((0,), (0,)), ((), ()))
ALONG = (((1,), (0,)), ((), ()))


def iota(shape, dim):
    return lax.broadcasted_iota(jnp.int32, shape, dim)


def in_three(x):
    hi = x.astype(jnp.bfloat16)
    rest = x - hi.astype(jnp.float32)
    mid = rest.astype(jnp.bfloat16)
    return hi, mid, (rest - mid.astype(jnp.float32)).astype(jnp.bfloat16)


def dot32(a, b, dims):
    return lax.dot_general(a, b, dims, preferred_element_type=jnp.float32)


def dot_exact(a, b, dims):
    return lax.dot_general(a, b, dims, precision=EXACT, preferred_element_type=jnp.float32)


def target_lane(cap):
    return -(-(cap + 2) // 8) * 8


def packed(pooled, reward):
    terms = [term.astype(jnp.float32) for term in in_three(reward)]
    terms.append(jnp.zeros((reward.shape[0], LANES - 3 * SIDE), jnp.float32))
    side = jnp.concatenate(terms, axis=1)
    return jnp.concatenate([pooled, side], axis=1).astype(jnp.bfloat16)


def rewards_of(side):
    return side[:, :SIDE] + side[:, SIDE : 2 * SIDE] + side[:, 2 * SIDE : 3 * SIDE]


def padded(ref, scratch):
    scratch[...] = jnp.zeros_like(scratch)
    scratch[: ref.shape[0]] = ref[...]
    return scratch[...]


def flags_kernel(cap, length_ref, owner_ref, rows_ref, targets_ref, out_ref):
    groups = out_ref.shape[0]
    slots = rows_ref.shape[1]
    length = length_ref[0]
    live = (rows_ref[...] < length).astype(jnp.float32)
    slot = iota((groups, slots), 1)
    first = iota((groups, slots), 0) * cap
    mine = jnp.where((slot >= first) & (slot < first + cap), live, 0.0).astype(jnp.bfloat16)
    rank = lax.rem(iota((LANES, slots), 1), cap)
    place = (rank == iota((LANES, slots), 0)).astype(jnp.bfloat16)
    flags = dot32(mine, place, LAST)
    owned = (owner_ref[...] == iota((groups, owner_ref.shape[1]), 0)).astype(jnp.float32)
    count = jnp.sum(owned, axis=1, keepdims=True)
    lane = iota((groups, LANES), 1)
    flags = jnp.where(lane == cap, count, flags)
    out_ref[...] = jnp.where(lane == cap + 1, length.astype(jnp.float32), flags)
    first = target_lane(cap)
    objectives = targets_ref.shape[1]
    out_ref[:, first : first + objectives] = jnp.broadcast_to(
        targets_ref[...], (groups, objectives)
    )


def stats_kernel(
    after_ref,
    hidden_ref,
    weight_ref,
    text_ref,
    gain_ref,
    head_ref,
    visual_ref,
    stats_ref,
    hidden,
    weight,
    text,
    head,
    arrived,
):
    chunks, tokens, depth = hidden.shape
    objectives = head_ref.shape[0]
    copies = [pltpu.make_async_copy(text_ref, text, arrived.at[0])]
    for i in range(chunks):
        part = pl.ds(i * depth, depth)
        copies.append(
            pltpu.make_async_copy(hidden_ref.at[:, part], hidden.at[i], arrived.at[2 * i + 1])
        )
        copies.append(
            pltpu.make_async_copy(weight_ref.at[part, :], weight.at[i], arrived.at[2 * i + 2])
        )
    for copy in copies:
        copy.start()
    gained = jnp.concatenate(in_three(gain_ref[...] * padded(head_ref, head)), axis=0)

    def of_rows(x):
        parts = dot32(gained, x, LAST)
        value = parts[:K_ROWS] + parts[K_ROWS : 2 * K_ROWS] + parts[2 * K_ROWS :]
        wide = x.astype(jnp.float32)
        square = wide * wide
        high = square.astype(jnp.bfloat16)
        low = (square - high.astype(jnp.float32)).astype(jnp.bfloat16)
        ones = jnp.ones((K_ROWS, x.shape[1]), jnp.bfloat16)
        squares = dot32(ones, high, LAST) + dot32(ones, low, LAST)
        return jnp.where(iota(value.shape, 0) == objectives, squares, value)

    copies[0].wait()
    stats_ref[:, tokens:] = of_rows(text[...])
    total = None
    for i in range(chunks):
        copies[2 * i + 1].wait()
        copies[2 * i + 2].wait()
        part = dot32(hidden[i], weight[i], ALONG)
        total = part if total is None else total + part
    visual = total.astype(jnp.bfloat16)
    visual_ref[...] = visual
    stats_ref[:, :tokens] = of_rows(visual)


def pooled_kernel(
    cap,
    objectives,
    features,
    me_ref,
    length_ref,
    stats_ref,
    flags_ref,
    owner_ref,
    rows_ref,
    visual_ref,
    text_ref,
    pooled_ref,
    kept_ref,
):
    tokens, width = visual_ref.shape
    positions = text_ref.shape[0]
    groups = flags_ref.shape[0]
    slots = rows_ref.shape[1]
    stats = stats_ref[0]
    for part in range(1, stats_ref.shape[0]):
        stats = stats + stats_ref[part]
    inv = lax.rsqrt(stats[objectives : objectives + 1] / features + EPSILON)
    flags = flags_ref[...]

    owned = owner_ref[...] == iota((groups, tokens), 0)
    member = owned.astype(jnp.bfloat16)
    before = (iota((tokens, tokens), 0) < iota((tokens, tokens), 1)).astype(jnp.bfloat16)
    earlier = dot32(member, before, ALONG)
    rank = jnp.sum(jnp.where(owned, earlier, 0.0), axis=0, keepdims=True)
    told = dot_exact(flags, owned.astype(jnp.float32), FIRST)
    at = iota(told.shape, 0)
    live = jnp.sum(
        jnp.where((at < cap) & (at == rank.astype(jnp.int32)), told, 0.0), axis=0, keepdims=True
    )
    token_inv = inv[:, :tokens]
    token_weight = live * token_inv / told[cap + 1 : cap + 2]

    length = length_ref[0]
    slot = iota((groups, slots), 1)
    first = iota((groups, slots), 0) * cap
    count = flags[:, cap : cap + 1].astype(jnp.int32)
    used = jnp.sum(((slot >= first) & (slot < first + count)).astype(jnp.float32), axis=0, keepdims=True)
    row = rows_ref[...]
    tall = positions // LANES
    high = jnp.where(lax.div(row, LANES) == iota((tall, slots), 0), used, 0.0).astype(jnp.bfloat16)
    low = (lax.rem(row, LANES) == iota((LANES, slots), 0)).astype(jnp.bfloat16)
    replaced = dot32(high, low, LAST)
    replaced = jnp.concatenate([replaced[i : i + 1] for i in range(tall)], axis=1)
    stays = (iota((1, positions), 1) < length) & (replaced < 0.5)
    text_weight = jnp.where(stays, inv[:, tokens:], 0.0) / length.astype(jnp.float32)

    spread = jnp.where(owned, token_weight, 0.0)
    three = dot32(jnp.concatenate(in_three(spread), axis=0), visual_ref[...], ALONG)
    pooled = three[:groups] + three[groups : 2 * groups] + three[2 * groups :]
    reward = dot_exact(spread, stats[:, :tokens], LAST)
    split = jnp.concatenate(in_three(jnp.broadcast_to(text_weight, (16, positions))), axis=0)
    text_three = dot32(split, text_ref[...], ALONG)
    text_pooled = text_three[0:1] + text_three[16:17] + text_three[32:33]
    text_reward = dot_exact(
        jnp.broadcast_to(text_weight, (8, positions)), stats[:, tokens:], LAST
    )[0:1]
    mine = iota((groups, 1), 0) == me_ref[0]
    pooled_ref[:, :width] = pooled + jnp.where(mine, text_pooled, 0.0)
    reward = reward + jnp.where(mine, text_reward, 0.0)
    pooled_ref[:, width:] = jnp.zeros((groups, LANES), jnp.float32)
    pooled_ref[:, width : width + objectives] = reward[:, :objectives]
    kept = jnp.where(iota((K_ROWS, tokens), 0) == objectives, token_weight, stats[:, :tokens])
    factor = token_weight * token_inv * token_inv / features
    kept_ref[...] = jnp.where(iota((K_ROWS, tokens), 0) == objectives + 1, factor, kept)


def fold_kernel(parts_ref, out_ref):
    total = parts_ref[0].astype(jnp.float32)
    for part in range(1, parts_ref.shape[0]):
        total = total + parts_ref[part].astype(jnp.float32)
    width = total.shape[1] - LANES
    joined, side = total[:, :width], total[:, width:]
    if out_ref.dtype == jnp.bfloat16:
        once = packed(joined, side[:, :SIDE])
    else:
        spare = jnp.zeros((side.shape[0], LANES - SIDE), jnp.float32)
        once = jnp.concatenate([joined, rewards_of(side), spare], axis=1)
    for copy in range(out_ref.shape[0]):
        out_ref[copy] = once


def grads_kernel(
    cap,
    scale,
    me_ref,
    pooled_ref,
    kept_ref,
    flags_ref,
    owner_ref,
    visual_ref,
    labels_ref,
    gain_ref,
    head_ref,
    reward_ref,
    visual_grad_ref,
    head_grad_ref,
    gain_grad_ref,
    marks,
    head_all,
):
    tokens, width = visual_ref.shape
    groups = flags_ref.shape[0]
    objectives = labels_ref.shape[0]
    z = pooled_ref[:, :width]
    rest = pooled_ref[:, width:]
    mine = iota(rest.shape, 0) == me_ref[0]
    reward_ref[...] = jnp.sum(jnp.where(mine, rest, 0.0), axis=0, keepdims=True)
    first = target_lane(cap)
    error = rest.T[:K_ROWS] - flags_ref[...].T[first : first + K_ROWS]
    labels = padded(labels_ref, marks).astype(jnp.float32)
    count = jnp.maximum(jnp.sum(labels, axis=1, keepdims=True), 1.0)
    cot = scale * labels * error / count
    gain = gain_ref[...]
    head = padded(head_ref, head_all)
    head_grad_ref[...] = (gain * dot_exact(cot, z, ALONG))[:objectives]
    direction = dot_exact(cot, head, FIRST)
    gain_grad_ref[...] = jnp.sum(z * direction, axis=0, keepdims=True)
    owned = owner_ref[...] == iota((groups, tokens), 0)
    kept = kept_ref[...]
    own_cot = dot_exact(cot, owned.astype(jnp.float32), ALONG)
    is_value = iota(kept.shape, 0) < objectives
    row_dot = jnp.sum(jnp.where(is_value, kept * own_cot, 0.0), axis=0, keepdims=True)
    weight = kept[objectives : objectives + 1]
    beta = kept[objectives + 1 : objectives + 2] * row_dot
    both = jnp.concatenate([weight, beta, jnp.zeros((LANES - 2, tokens), jnp.float32)], axis=0)
    columns = both.T
    member = owned.astype(jnp.bfloat16)
    directions = jnp.concatenate(in_three(gain * direction), axis=0)
    own = dot32(jnp.concatenate([member] * 3, axis=0), directions, FIRST)
    grad = columns[:, 0:1] * own - columns[:, 1:2] * visual_ref[...].astype(jnp.float32)
    visual_grad_ref[...] = grad.astype(jnp.bfloat16)


def whole(count):
    return [pl.BlockSpec(memory_space=pltpu.VMEM)] * count


def in_hbm(array):
    return pltpu.with_memory_space_constraint(array, pltpu.HBM)


def scalars(count):
    return [pl.BlockSpec(memory_space=pltpu.SMEM)] * count


def folded(parts, copies, kind, name):
    return pl.pallas_call(
        fold_kernel,
        out_shape=jax.ShapeDtypeStruct((copies, *parts.shape[1:]), kind),
        in_specs=whole(1),
        out_specs=pl.BlockSpec(memory_space=pltpu.VMEM),
        compiler_params=VMEM,
        name=f"fold_{name}",
    )(parts)


def on_device(
    hidden, merge_weight, text_embed, gain, head_weight, owner, vis_row, lengths, labels, targets
):
    groups, near = lax.axis_size(GRP), lax.axis_size(NEAR)
    tokens, depth = hidden.shape
    positions, width = text_embed.shape
    objectives = head_weight.shape[1]
    cap = vis_row.shape[1] // groups
    features = float(width * lax.axis_size(TP))
    scale = float(positions * groups // 16)
    me = lax.axis_index(GRP).astype(jnp.int32).reshape(1)
    owners = owner.reshape(1, tokens)
    gain_row = gain.reshape(1, width)
    head = head_weight.T
    marks = labels.T

    flags = pl.pallas_call(
        functools.partial(flags_kernel, cap),
        out_shape=jax.ShapeDtypeStruct((groups, LANES), jnp.float32),
        in_specs=scalars(1) + whole(3),
        out_specs=pl.BlockSpec(memory_space=pltpu.VMEM),
        compiler_params=VMEM,
        name="flags",
    )(lengths, in_hbm(owners), in_hbm(vis_row), in_hbm(targets))
    told = lax.all_to_all(
        flags.reshape(groups, 1, LANES), GRP, split_axis=0, concat_axis=0, tiled=True
    ).reshape(groups, LANES)

    chunks = 5
    rows = tokens + positions
    visual, stats = pl.pallas_call(
        stats_kernel,
        out_shape=(
            jax.ShapeDtypeStruct((tokens, width), jnp.bfloat16),
            jax.ShapeDtypeStruct((K_ROWS, rows), jnp.float32),
        ),
        in_specs=[pl.BlockSpec(memory_space=pl.ANY)]
        + [pl.BlockSpec(memory_space=pltpu.HBM)] * 3
        + whole(2),
        out_specs=tuple(whole(2)),
        scratch_shapes=[
            pltpu.VMEM((chunks, tokens, depth // chunks), jnp.bfloat16),
            pltpu.VMEM((chunks, depth // chunks, width), jnp.bfloat16),
            pltpu.VMEM((positions, width), jnp.bfloat16),
            pltpu.VMEM((K_ROWS, width), jnp.float32),
            pltpu.SemaphoreType.DMA((2 * chunks + 1,)),
        ],
        compiler_params=VMEM,
        name="stats",
    )(flags, in_hbm(hidden), in_hbm(merge_weight), in_hbm(text_embed), in_hbm(gain_row), in_hbm(head))
    stats = lax.all_gather(jnp.sum(lax.all_gather(stats, "tx"), axis=0), "ty")

    pooled, kept = pl.pallas_call(
        functools.partial(pooled_kernel, cap, objectives, features),
        out_shape=(
            jax.ShapeDtypeStruct((groups, width + LANES), jnp.float32),
            jax.ShapeDtypeStruct((K_ROWS, tokens), jnp.float32),
        ),
        in_specs=scalars(2) + whole(6),
        out_specs=tuple(whole(2)),
        compiler_params=VMEM,
        name="pooled",
    )(me, lengths, stats, told, owners, vis_row, visual, text_embed)
    block = pooled.reshape(near, groups // near, width + LANES)
    block = lax.all_to_all(block, NEAR, split_axis=0, concat_axis=0, tiled=True)
    block = folded(block, lax.axis_size("far"), jnp.bfloat16, "near")
    block = lax.all_to_all(block, "far", split_axis=0, concat_axis=0, tiled=True)
    block = folded(block, near, jnp.float32, "far")
    block = lax.all_to_all(block, NEAR, split_axis=0, concat_axis=0, tiled=True)
    pooled = block.reshape(groups, width + LANES)

    reward, visual_grad, head_grad, gain_grad = pl.pallas_call(
        functools.partial(grads_kernel, cap, scale),
        out_shape=(
            jax.ShapeDtypeStruct((1, LANES), jnp.float32),
            jax.ShapeDtypeStruct((tokens, width), jnp.bfloat16),
            jax.ShapeDtypeStruct((objectives, width), jnp.float32),
            jax.ShapeDtypeStruct((1, width), jnp.float32),
        ),
        in_specs=scalars(1) + whole(8),
        out_specs=tuple(whole(4)),
        scratch_shapes=[
            pltpu.VMEM((K_ROWS, groups), jnp.int32),
            pltpu.VMEM((K_ROWS, width), jnp.float32),
        ],
        compiler_params=VMEM,
        name="grads",
    )(me, pooled, kept, told, owners, visual, marks, gain_row, head)
    return reward[:, :objectives], visual_grad, head_grad.T, gain_grad.reshape(width)


def solution(mesh):
    groups, tp = mesh.shape["grp"], mesh.shape["tp"]
    near = 4 if groups % 16 == 0 else 2
    ty = 4 if tp % 16 == 0 else 1
    torus = Mesh(
        mesh.devices.reshape(groups // (2 * near), near, 2, ty, tp // ty),
        ("far", "near", "core", "ty", "tx"),
    )
    placed = (
        P(GRP, None),
        P(None, TP),
        P(GRP, TP),
        P(TP),
        P(TP, None),
        P(GRP, None),
        P(GRP, None),
        P(GRP),
        P(),
        P(GRP, None),
    )
    return jax.shard_map(
        on_device,
        mesh=torus,
        in_specs=placed,
        out_specs=(P(GRP, None), P(GRP, TP), P(TP, None), P(TP)),
        check_vma=False,
    )
```

```python
import functools

import jax
import jax.numpy as jnp
from jax import lax
from jax.experimental import pallas as pl
from jax.experimental.pallas import tpu as pltpu
from jax.sharding import Mesh
from jax.sharding import PartitionSpec as P

GRP = ("far", "near", "core")
NEAR = ("near", "core")
TP = ("ty", "tx")
EPSILON = 1e-06
LANES = 128
K_ROWS = 24
SIDE = 32
VMEM = pltpu.CompilerParams(vmem_limit_bytes=48 * 2**20)
EXACT = lax.Precision.HIGHEST
LAST = (((1,), (1,)), ((), ()))
FIRST = (((0,), (0,)), ((), ()))
ALONG = (((1,), (0,)), ((), ()))


def iota(shape, dim):
    return lax.broadcasted_iota(jnp.int32, shape, dim)


def in_three(x):
    hi = x.astype(jnp.bfloat16)
    rest = x - hi.astype(jnp.float32)
    mid = rest.astype(jnp.bfloat16)
    return hi, mid, (rest - mid.astype(jnp.float32)).astype(jnp.bfloat16)


def dot32(a, b, dims):
    return lax.dot_general(a, b, dims, preferred_element_type=jnp.float32)


def dot_exact(a, b, dims):
    return lax.dot_general(a, b, dims, precision=EXACT, preferred_element_type=jnp.float32)


def target_lane(cap):
    return -(-(cap + 2) // 8) * 8


def packed(pooled, reward):
    terms = [term.astype(jnp.float32) for term in in_three(reward)]
    terms.append(jnp.zeros((reward.shape[0], LANES - 3 * SIDE), jnp.float32))
    side = jnp.concatenate(terms, axis=1)
    return jnp.concatenate([pooled, side], axis=1).astype(jnp.bfloat16)


def rewards_of(side):
    return side[:, :SIDE] + side[:, SIDE : 2 * SIDE] + side[:, 2 * SIDE : 3 * SIDE]


def padded(ref, scratch):
    scratch[...] = jnp.zeros_like(scratch)
    scratch[: ref.shape[0]] = ref[...]
    return scratch[...]


def tight_lanes(rows):
    return -(-rows // (2 * LANES)) * LANES


def tight(stats):
    rows = stats.shape[1]
    half = tight_lanes(rows)
    last = jnp.concatenate([stats[16:20, :half], stats[16:20, rows - half :]], axis=0)
    return jnp.concatenate([stats[:8], stats[8:16], last], axis=1)


def loose(packed_stats, rows):
    half = tight_lanes(rows)
    last = packed_stats[:, 2 * rows :]
    last = jnp.concatenate([last[:4, :half], last[4:, 2 * half - rows :]], axis=1)
    last = jnp.concatenate([last, jnp.zeros_like(last)], axis=0)
    return jnp.concatenate([packed_stats[:, :rows], packed_stats[:, rows : 2 * rows], last], axis=0)


def flags_kernel(cap, length_ref, owner_ref, rows_ref, targets_ref, out_ref):
    groups = out_ref.shape[0]
    slots = rows_ref.shape[1]
    length = length_ref[0]
    live = (rows_ref[...] < length).astype(jnp.float32)
    slot = iota((groups, slots), 1)
    first = iota((groups, slots), 0) * cap
    mine = jnp.where((slot >= first) & (slot < first + cap), live, 0.0).astype(jnp.bfloat16)
    rank = lax.rem(iota((LANES, slots), 1), cap)
    place = (rank == iota((LANES, slots), 0)).astype(jnp.bfloat16)
    flags = dot32(mine, place, LAST)
    owned = (owner_ref[...] == iota((groups, owner_ref.shape[1]), 0)).astype(jnp.float32)
    count = jnp.sum(owned, axis=1, keepdims=True)
    lane = iota((groups, LANES), 1)
    flags = jnp.where(lane == cap, count, flags)
    out_ref[...] = jnp.where(lane == cap + 1, length.astype(jnp.float32), flags)
    first = target_lane(cap)
    objectives = targets_ref.shape[1]
    out_ref[:, first : first + objectives] = jnp.broadcast_to(
        targets_ref[...], (groups, objectives)
    )


def stats_kernel(
    after_ref,
    hidden_ref,
    weight_ref,
    text_ref,
    gain_ref,
    head_ref,
    visual_ref,
    stats_ref,
    hidden,
    weight,
    text,
    head,
    arrived,
):
    chunks, tokens, depth = hidden.shape
    objectives = head_ref.shape[0]
    copies = [pltpu.make_async_copy(text_ref, text, arrived.at[0])]
    for i in range(chunks):
        part = pl.ds(i * depth, depth)
        copies.append(
            pltpu.make_async_copy(hidden_ref.at[:, part], hidden.at[i], arrived.at[2 * i + 1])
        )
        copies.append(
            pltpu.make_async_copy(weight_ref.at[part, :], weight.at[i], arrived.at[2 * i + 2])
        )
    for copy in copies:
        copy.start()
    gained = jnp.concatenate(in_three(gain_ref[...] * padded(head_ref, head)), axis=0)

    def of_rows(x):
        parts = dot32(gained, x, LAST)
        value = parts[:K_ROWS] + parts[K_ROWS : 2 * K_ROWS] + parts[2 * K_ROWS :]
        wide = x.astype(jnp.float32)
        square = wide * wide
        lanes = square[:, :LANES]
        for at in range(LANES, x.shape[1], LANES):
            lanes = lanes + square[:, at : at + LANES]
        terms = jnp.concatenate(in_three(lanes), axis=1)
        squares = dot32(jnp.ones((K_ROWS, terms.shape[1]), jnp.bfloat16), terms, LAST)
        return jnp.where(iota(value.shape, 0) == objectives, squares, value)

    copies[0].wait()
    of_text = of_rows(text[...])
    total = None
    for i in range(chunks):
        copies[2 * i + 1].wait()
        copies[2 * i + 2].wait()
        part = dot32(hidden[i], weight[i], ALONG)
        total = part if total is None else total + part
    visual = total.astype(jnp.bfloat16)
    visual_ref[...] = visual
    stats_ref[...] = tight(jnp.concatenate([of_rows(visual), of_text], axis=1))


def pooled_kernel(
    cap,
    objectives,
    features,
    me_ref,
    length_ref,
    stats_ref,
    flags_ref,
    owner_ref,
    rows_ref,
    visual_ref,
    text_ref,
    pooled_ref,
    kept_ref,
):
    tokens, width = visual_ref.shape
    positions = text_ref.shape[0]
    groups = flags_ref.shape[0]
    slots = rows_ref.shape[1]
    stats = stats_ref[0]
    for part in range(1, stats_ref.shape[0]):
        stats = stats + stats_ref[part]
    stats = loose(stats, tokens + positions)
    inv = lax.rsqrt(stats[objectives : objectives + 1] / features + EPSILON)
    flags = flags_ref[...]

    owned = owner_ref[...] == iota((groups, tokens), 0)
    member = owned.astype(jnp.bfloat16)
    before = (iota((tokens, tokens), 0) < iota((tokens, tokens), 1)).astype(jnp.bfloat16)
    earlier = dot32(member, before, ALONG)
    rank = jnp.sum(jnp.where(owned, earlier, 0.0), axis=0, keepdims=True)
    told = dot_exact(flags, owned.astype(jnp.float32), FIRST)
    at = iota(told.shape, 0)
    live = jnp.sum(
        jnp.where((at < cap) & (at == rank.astype(jnp.int32)), told, 0.0), axis=0, keepdims=True
    )
    token_inv = inv[:, :tokens]
    token_weight = live * token_inv / told[cap + 1 : cap + 2]

    length = length_ref[0]
    slot = iota((groups, slots), 1)
    first = iota((groups, slots), 0) * cap
    count = flags[:, cap : cap + 1].astype(jnp.int32)
    used = jnp.sum(((slot >= first) & (slot < first + count)).astype(jnp.float32), axis=0, keepdims=True)
    row = rows_ref[...]
    tall = positions // LANES
    high = jnp.where(lax.div(row, LANES) == iota((tall, slots), 0), used, 0.0).astype(jnp.bfloat16)
    low = (lax.rem(row, LANES) == iota((LANES, slots), 0)).astype(jnp.bfloat16)
    replaced = dot32(high, low, LAST)
    replaced = jnp.concatenate([replaced[i : i + 1] for i in range(tall)], axis=1)
    stays = (iota((1, positions), 1) < length) & (replaced < 0.5)
    text_weight = jnp.where(stays, inv[:, tokens:], 0.0) / length.astype(jnp.float32)

    spread = jnp.where(owned, token_weight, 0.0)
    three = dot32(jnp.concatenate(in_three(spread), axis=0), visual_ref[...], ALONG)
    pooled = three[:groups] + three[groups : 2 * groups] + three[2 * groups :]
    reward = dot_exact(spread, stats[:, :tokens], LAST)
    split = jnp.concatenate(in_three(jnp.broadcast_to(text_weight, (16, positions))), axis=0)
    text_three = dot32(split, text_ref[...], ALONG)
    text_pooled = text_three[0:1] + text_three[16:17] + text_three[32:33]
    text_reward = dot_exact(
        jnp.broadcast_to(text_weight, (8, positions)), stats[:, tokens:], LAST
    )[0:1]
    mine = iota((groups, 1), 0) == me_ref[0]
    pooled_ref[:, :width] = pooled + jnp.where(mine, text_pooled, 0.0)
    reward = reward + jnp.where(mine, text_reward, 0.0)
    pooled_ref[:, width:] = jnp.zeros((groups, LANES), jnp.float32)
    pooled_ref[:, width : width + objectives] = reward[:, :objectives]
    kept = jnp.where(iota((K_ROWS, tokens), 0) == objectives, token_weight, stats[:, :tokens])
    factor = token_weight * token_inv * token_inv / features
    kept_ref[...] = jnp.where(iota((K_ROWS, tokens), 0) == objectives + 1, factor, kept)


def fold_kernel(parts_ref, out_ref):
    total = parts_ref[0].astype(jnp.float32)
    for part in range(1, parts_ref.shape[0]):
        total = total + parts_ref[part].astype(jnp.float32)
    width = total.shape[1] - LANES
    joined, side = total[:, :width], total[:, width:]
    if out_ref.dtype == jnp.bfloat16:
        once = packed(joined, side[:, :SIDE])
    else:
        spare = jnp.zeros((side.shape[0], LANES - SIDE), jnp.float32)
        once = jnp.concatenate([joined, rewards_of(side), spare], axis=1)
    for copy in range(out_ref.shape[0]):
        out_ref[copy] = once


def grads_kernel(
    cap,
    scale,
    me_ref,
    pooled_ref,
    kept_ref,
    flags_ref,
    owner_ref,
    visual_ref,
    labels_ref,
    gain_ref,
    head_ref,
    reward_ref,
    visual_grad_ref,
    head_grad_ref,
    gain_grad_ref,
    marks,
    head_all,
):
    tokens, width = visual_ref.shape
    groups = flags_ref.shape[0]
    objectives = labels_ref.shape[0]
    z = pooled_ref[:, :width]
    rest = pooled_ref[:, width:]
    mine = iota(rest.shape, 0) == me_ref[0]
    reward_ref[...] = jnp.sum(jnp.where(mine, rest, 0.0), axis=0, keepdims=True)
    first = target_lane(cap)
    error = rest.T[:K_ROWS] - flags_ref[...].T[first : first + K_ROWS]
    labels = padded(labels_ref, marks).astype(jnp.float32)
    count = jnp.maximum(jnp.sum(labels, axis=1, keepdims=True), 1.0)
    cot = scale * labels * error / count
    gain = gain_ref[...]
    head = padded(head_ref, head_all)
    head_grad_ref[...] = (gain * dot_exact(cot, z, ALONG))[:objectives]
    direction = dot_exact(cot, head, FIRST)
    gain_grad_ref[...] = jnp.sum(z * direction, axis=0, keepdims=True)
    owned = owner_ref[...] == iota((groups, tokens), 0)
    kept = kept_ref[...]
    own_cot = dot_exact(cot, owned.astype(jnp.float32), ALONG)
    is_value = iota(kept.shape, 0) < objectives
    row_dot = jnp.sum(jnp.where(is_value, kept * own_cot, 0.0), axis=0, keepdims=True)
    weight = kept[objectives : objectives + 1]
    beta = kept[objectives + 1 : objectives + 2] * row_dot
    both = jnp.concatenate([weight, beta, jnp.zeros((LANES - 2, tokens), jnp.float32)], axis=0)
    columns = both.T
    member = owned.astype(jnp.bfloat16)
    directions = jnp.concatenate(in_three(gain * direction), axis=0)
    own = dot32(jnp.concatenate([member] * 3, axis=0), directions, FIRST)
    grad = columns[:, 0:1] * own - columns[:, 1:2] * visual_ref[...].astype(jnp.float32)
    visual_grad_ref[...] = grad.astype(jnp.bfloat16)


def whole(count):
    return [pl.BlockSpec(memory_space=pltpu.VMEM)] * count


def in_hbm(array):
    return pltpu.with_memory_space_constraint(array, pltpu.HBM)


def scalars(count):
    return [pl.BlockSpec(memory_space=pltpu.SMEM)] * count


def folded(parts, copies, kind, name):
    return pl.pallas_call(
        fold_kernel,
        out_shape=jax.ShapeDtypeStruct((copies, *parts.shape[1:]), kind),
        in_specs=whole(1),
        out_specs=pl.BlockSpec(memory_space=pltpu.VMEM),
        compiler_params=VMEM,
        name=f"fold_{name}",
    )(parts)


def on_device(
    hidden, merge_weight, text_embed, gain, head_weight, owner, vis_row, lengths, labels, targets
):
    groups, near = lax.axis_size(GRP), lax.axis_size(NEAR)
    tokens, depth = hidden.shape
    positions, width = text_embed.shape
    objectives = head_weight.shape[1]
    cap = vis_row.shape[1] // groups
    features = float(width * lax.axis_size(TP))
    scale = float(positions * groups // 16)
    me = lax.axis_index(GRP).astype(jnp.int32).reshape(1)
    owners = owner.reshape(1, tokens)
    gain_row = gain.reshape(1, width)
    head = head_weight.T
    marks = labels.T

    flags = pl.pallas_call(
        functools.partial(flags_kernel, cap),
        out_shape=jax.ShapeDtypeStruct((groups, LANES), jnp.float32),
        in_specs=scalars(1) + whole(3),
        out_specs=pl.BlockSpec(memory_space=pltpu.VMEM),
        compiler_params=VMEM,
        name="flags",
    )(lengths, in_hbm(owners), in_hbm(vis_row), in_hbm(targets))
    told = lax.all_to_all(
        flags.reshape(groups, 1, LANES), GRP, split_axis=0, concat_axis=0, tiled=True
    ).reshape(groups, LANES)

    chunks = 5
    rows = tokens + positions
    visual, stats = pl.pallas_call(
        stats_kernel,
        out_shape=(
            jax.ShapeDtypeStruct((tokens, width), jnp.bfloat16),
            jax.ShapeDtypeStruct((8, 2 * rows + tight_lanes(rows)), jnp.float32),
        ),
        in_specs=[pl.BlockSpec(memory_space=pl.ANY)]
        + [pl.BlockSpec(memory_space=pltpu.HBM)] * 3
        + whole(2),
        out_specs=tuple(whole(2)),
        scratch_shapes=[
            pltpu.VMEM((chunks, tokens, depth // chunks), jnp.bfloat16),
            pltpu.VMEM((chunks, depth // chunks, width), jnp.bfloat16),
            pltpu.VMEM((positions, width), jnp.bfloat16),
            pltpu.VMEM((K_ROWS, width), jnp.float32),
            pltpu.SemaphoreType.DMA((2 * chunks + 1,)),
        ],
        compiler_params=VMEM,
        name="stats",
    )(flags, in_hbm(hidden), in_hbm(merge_weight), in_hbm(text_embed), in_hbm(gain_row), in_hbm(head))
    stats = lax.all_gather(jnp.sum(lax.all_gather(stats, "tx"), axis=0), "ty")

    pooled, kept = pl.pallas_call(
        functools.partial(pooled_kernel, cap, objectives, features),
        out_shape=(
            jax.ShapeDtypeStruct((groups, width + LANES), jnp.float32),
            jax.ShapeDtypeStruct((K_ROWS, tokens), jnp.float32),
        ),
        in_specs=scalars(2) + whole(6),
        out_specs=tuple(whole(2)),
        compiler_params=VMEM,
        name="pooled",
    )(me, lengths, stats, told, owners, vis_row, visual, text_embed)
    block = pooled.reshape(near, groups // near, width + LANES)
    block = lax.all_to_all(block, NEAR, split_axis=0, concat_axis=0, tiled=True)
    block = folded(block, lax.axis_size("far"), jnp.bfloat16, "near")
    block = lax.all_to_all(block, "far", split_axis=0, concat_axis=0, tiled=True)
    block = folded(block, near, jnp.float32, "far")
    block = lax.all_to_all(block, NEAR, split_axis=0, concat_axis=0, tiled=True)
    pooled = block.reshape(groups, width + LANES)

    reward, visual_grad, head_grad, gain_grad = pl.pallas_call(
        functools.partial(grads_kernel, cap, scale),
        out_shape=(
            jax.ShapeDtypeStruct((1, LANES), jnp.float32),
            jax.ShapeDtypeStruct((tokens, width), jnp.bfloat16),
            jax.ShapeDtypeStruct((objectives, width), jnp.float32),
            jax.ShapeDtypeStruct((1, width), jnp.float32),
        ),
        in_specs=scalars(1) + whole(8),
        out_specs=tuple(whole(4)),
        scratch_shapes=[
            pltpu.VMEM((K_ROWS, groups), jnp.int32),
            pltpu.VMEM((K_ROWS, width), jnp.float32),
        ],
        compiler_params=VMEM,
        name="grads",
    )(me, pooled, kept, told, owners, visual, marks, gain_row, head)
    return reward[:, :objectives], visual_grad, head_grad.T, gain_grad.reshape(width)


def solution(mesh):
    groups, tp = mesh.shape["grp"], mesh.shape["tp"]
    near = 4 if groups % 16 == 0 else 2
    ty = 4 if tp % 16 == 0 else 1
    torus = Mesh(
        mesh.devices.reshape(groups // (2 * near), near, 2, ty, tp // ty),
        ("far", "near", "core", "ty", "tx"),
    )
    placed = (
        P(GRP, None),
        P(None, TP),
        P(GRP, TP),
        P(TP),
        P(TP, None),
        P(GRP, None),
        P(GRP, None),
        P(GRP),
        P(),
        P(GRP, None),
    )
    return jax.shard_map(
        on_device,
        mesh=torus,
        in_specs=placed,
        out_specs=(P(GRP, None), P(GRP, TP), P(TP, None), P(TP)),
        check_vma=False,
    )
```

```python
import functools

import jax
import jax.numpy as jnp
from jax import lax
from jax.experimental import pallas as pl
from jax.experimental.pallas import tpu as pltpu
from jax.sharding import Mesh
from jax.sharding import PartitionSpec as P

GRP = ("far", "near", "core")
NEAR = ("near", "core")
TP = ("ty", "tx")
EPSILON = 1e-06
LANES = 128
K_ROWS = 24
SIDE = 32
VMEM = pltpu.CompilerParams(vmem_limit_bytes=48 * 2**20)
EXACT = lax.Precision.HIGHEST
LAST = (((1,), (1,)), ((), ()))
FIRST = (((0,), (0,)), ((), ()))
ALONG = (((1,), (0,)), ((), ()))


def iota(shape, dim):
    return lax.broadcasted_iota(jnp.int32, shape, dim)


def in_three(x):
    hi = x.astype(jnp.bfloat16)
    rest = x - hi.astype(jnp.float32)
    mid = rest.astype(jnp.bfloat16)
    return hi, mid, (rest - mid.astype(jnp.float32)).astype(jnp.bfloat16)


def dot32(a, b, dims):
    return lax.dot_general(a, b, dims, preferred_element_type=jnp.float32)


def dot_exact(a, b, dims):
    return lax.dot_general(a, b, dims, precision=EXACT, preferred_element_type=jnp.float32)


def target_lane(cap):
    return -(-(cap + 2) // 8) * 8


def packed(pooled, reward):
    terms = [term.astype(jnp.float32) for term in in_three(reward)]
    terms.append(jnp.zeros((reward.shape[0], LANES - 3 * SIDE), jnp.float32))
    side = jnp.concatenate(terms, axis=1)
    return jnp.concatenate([pooled, side], axis=1).astype(jnp.bfloat16)


def rewards_of(side):
    return side[:, :SIDE] + side[:, SIDE : 2 * SIDE] + side[:, 2 * SIDE : 3 * SIDE]


def padded(ref, scratch):
    scratch[...] = jnp.zeros_like(scratch)
    scratch[: ref.shape[0]] = ref[...]
    return scratch[...]


def tight_lanes(rows):
    return -(-rows // (2 * LANES)) * LANES


def tight(stats):
    rows = stats.shape[1]
    half = tight_lanes(rows)
    last = jnp.concatenate([stats[16:20, :half], stats[16:20, rows - half :]], axis=0)
    return jnp.concatenate([stats[:8], stats[8:16], last], axis=1)


def loose(packed_stats, rows):
    half = tight_lanes(rows)
    last = packed_stats[:, 2 * rows :]
    last = jnp.concatenate([last[:4, :half], last[4:, 2 * half - rows :]], axis=1)
    last = jnp.concatenate([last, jnp.zeros_like(last)], axis=0)
    return jnp.concatenate([packed_stats[:, :rows], packed_stats[:, rows : 2 * rows], last], axis=0)


def flags_kernel(cap, length_ref, owner_ref, rows_ref, targets_ref, out_ref):
    groups = out_ref.shape[0]
    slots = rows_ref.shape[1]
    length = length_ref[0]
    live = (rows_ref[...] < length).astype(jnp.float32)
    slot = iota((groups, slots), 1)
    first = iota((groups, slots), 0) * cap
    mine = jnp.where((slot >= first) & (slot < first + cap), live, 0.0).astype(jnp.bfloat16)
    rank = lax.rem(iota((LANES, slots), 1), cap)
    place = (rank == iota((LANES, slots), 0)).astype(jnp.bfloat16)
    flags = dot32(mine, place, LAST)
    owned = (owner_ref[...] == iota((groups, owner_ref.shape[1]), 0)).astype(jnp.float32)
    count = jnp.sum(owned, axis=1, keepdims=True)
    lane = iota((groups, LANES), 1)
    flags = jnp.where(lane == cap, count, flags)
    out_ref[...] = jnp.where(lane == cap + 1, length.astype(jnp.float32), flags)
    first = target_lane(cap)
    objectives = targets_ref.shape[1]
    out_ref[:, first : first + objectives] = jnp.broadcast_to(
        targets_ref[...], (groups, objectives)
    )


def stats_kernel(
    after_ref,
    hidden_ref,
    weight_ref,
    text_ref,
    gain_ref,
    head_ref,
    visual_ref,
    stats_ref,
    hidden,
    weight,
    text,
    head,
    arrived,
):
    chunks, tokens, depth = hidden.shape
    objectives = head_ref.shape[0]
    copies = [pltpu.make_async_copy(text_ref, text, arrived.at[0])]
    for i in range(chunks):
        part = pl.ds(i * depth, depth)
        copies.append(
            pltpu.make_async_copy(hidden_ref.at[:, part], hidden.at[i], arrived.at[2 * i + 1])
        )
        copies.append(
            pltpu.make_async_copy(weight_ref.at[part, :], weight.at[i], arrived.at[2 * i + 2])
        )
    for copy in copies:
        copy.start()
    gained = jnp.concatenate(in_three(gain_ref[...] * padded(head_ref, head)), axis=0)

    def of_rows(x):
        parts = dot32(gained, x, LAST)
        value = parts[:K_ROWS] + parts[K_ROWS : 2 * K_ROWS] + parts[2 * K_ROWS :]
        wide = x.astype(jnp.float32)
        square = wide * wide
        lanes = square[:, :LANES]
        for at in range(LANES, x.shape[1], LANES):
            lanes = lanes + square[:, at : at + LANES]
        terms = jnp.concatenate(in_three(lanes), axis=1)
        squares = dot32(jnp.ones((K_ROWS, terms.shape[1]), jnp.bfloat16), terms, LAST)
        return jnp.where(iota(value.shape, 0) == objectives, squares, value)

    copies[0].wait()
    of_text = of_rows(text[...])
    total = None
    for i in range(chunks):
        copies[2 * i + 1].wait()
        copies[2 * i + 2].wait()
        part = dot32(hidden[i], weight[i], ALONG)
        total = part if total is None else total + part
    visual = total.astype(jnp.bfloat16)
    visual_ref[...] = visual
    stats_ref[...] = tight(jnp.concatenate([of_rows(visual), of_text], axis=1))


def pooled_kernel(
    cap,
    objectives,
    features,
    me_ref,
    length_ref,
    stats_ref,
    flags_ref,
    owner_ref,
    rows_ref,
    visual_ref,
    text_ref,
    pooled_ref,
    kept_ref,
):
    tokens, width = visual_ref.shape
    positions = text_ref.shape[0]
    groups = flags_ref.shape[0]
    slots = rows_ref.shape[1]
    stats = stats_ref[0]
    for part in range(1, stats_ref.shape[0]):
        stats = stats + stats_ref[part]
    stats = loose(stats, tokens + positions)
    inv = lax.rsqrt(stats[objectives : objectives + 1] / features + EPSILON)
    flags = flags_ref[...]

    owned = owner_ref[...] == iota((groups, tokens), 0)
    member = owned.astype(jnp.bfloat16)
    before = (iota((tokens, tokens), 0) < iota((tokens, tokens), 1)).astype(jnp.bfloat16)
    earlier = dot32(member, before, ALONG)
    rank = jnp.sum(jnp.where(owned, earlier, 0.0), axis=0, keepdims=True)
    told = dot_exact(flags, owned.astype(jnp.float32), FIRST)
    at = iota(told.shape, 0)
    live = jnp.sum(
        jnp.where((at < cap) & (at == rank.astype(jnp.int32)), told, 0.0), axis=0, keepdims=True
    )
    token_inv = inv[:, :tokens]
    token_weight = live * token_inv / told[cap + 1 : cap + 2]

    length = length_ref[0]
    slot = iota((groups, slots), 1)
    first = iota((groups, slots), 0) * cap
    count = flags[:, cap : cap + 1].astype(jnp.int32)
    used = jnp.sum(((slot >= first) & (slot < first + count)).astype(jnp.float32), axis=0, keepdims=True)
    row = rows_ref[...]
    tall = positions // LANES
    high = jnp.where(lax.div(row, LANES) == iota((tall, slots), 0), used, 0.0).astype(jnp.bfloat16)
    low = (lax.rem(row, LANES) == iota((LANES, slots), 0)).astype(jnp.bfloat16)
    replaced = dot32(high, low, LAST)
    replaced = jnp.concatenate([replaced[i : i + 1] for i in range(tall)], axis=1)
    stays = (iota((1, positions), 1) < length) & (replaced < 0.5)
    text_weight = jnp.where(stays, inv[:, tokens:], 0.0) / length.astype(jnp.float32)

    spread = jnp.where(owned, token_weight, 0.0)
    three = dot32(jnp.concatenate(in_three(spread), axis=0), visual_ref[...], ALONG)
    pooled = three[:groups] + three[groups : 2 * groups] + three[2 * groups :]
    reward = dot_exact(spread, stats[:, :tokens], LAST)
    split = jnp.concatenate(in_three(jnp.broadcast_to(text_weight, (16, positions))), axis=0)
    text_three = dot32(split, text_ref[...], ALONG)
    text_pooled = text_three[0:1] + text_three[16:17] + text_three[32:33]
    text_reward = dot_exact(
        jnp.broadcast_to(text_weight, (8, positions)), stats[:, tokens:], LAST
    )[0:1]
    mine = iota((groups, 1), 0) == me_ref[0]
    pooled_ref[:, :width] = pooled + jnp.where(mine, text_pooled, 0.0)
    reward = reward + jnp.where(mine, text_reward, 0.0)
    pooled_ref[:, width:] = jnp.zeros((groups, LANES), jnp.float32)
    pooled_ref[:, width : width + objectives] = reward[:, :objectives]
    kept = jnp.where(iota((K_ROWS, tokens), 0) == objectives, token_weight, stats[:, :tokens])
    factor = token_weight * token_inv * token_inv / features
    kept_ref[...] = jnp.where(iota((K_ROWS, tokens), 0) == objectives + 1, factor, kept)


def fold_kernel(parts_ref, out_ref):
    total = parts_ref[0].astype(jnp.float32)
    for part in range(1, parts_ref.shape[0]):
        total = total + parts_ref[part].astype(jnp.float32)
    width = total.shape[1] - LANES
    joined, side = total[:, :width], total[:, width:]
    if out_ref.dtype == jnp.bfloat16:
        once = packed(joined, side[:, :SIDE])
    else:
        spare = jnp.zeros((side.shape[0], LANES - SIDE), jnp.float32)
        once = jnp.concatenate([joined, rewards_of(side), spare], axis=1)
    for copy in range(out_ref.shape[0]):
        out_ref[copy] = once


def grads_kernel(
    cap,
    scale,
    me_ref,
    pooled_ref,
    kept_ref,
    flags_ref,
    owner_ref,
    visual_ref,
    labels_ref,
    gain_ref,
    head_ref,
    reward_ref,
    visual_grad_ref,
    head_grad_ref,
    gain_grad_ref,
    marks,
    head_all,
):
    tokens, width = visual_ref.shape
    groups = flags_ref.shape[0]
    objectives = labels_ref.shape[0]
    z = pooled_ref[:, :width]
    rest = pooled_ref[:, width:]
    mine = iota(rest.shape, 0) == me_ref[0]
    reward_ref[...] = jnp.sum(jnp.where(mine, rest, 0.0), axis=0, keepdims=True)
    first = target_lane(cap)
    error = rest.T[:K_ROWS] - flags_ref[...].T[first : first + K_ROWS]
    labels = padded(labels_ref, marks).astype(jnp.float32)
    count = jnp.maximum(jnp.sum(labels, axis=1, keepdims=True), 1.0)
    cot = scale * labels * error / count
    gain = gain_ref[...]
    head = padded(head_ref, head_all)
    head_grad_ref[...] = (gain * dot_exact(cot, z, ALONG))[:objectives]
    direction = dot_exact(cot, head, FIRST)
    gain_grad_ref[...] = jnp.sum(z * direction, axis=0, keepdims=True)
    owned = owner_ref[...] == iota((groups, tokens), 0)
    kept = kept_ref[...]
    own_cot = dot_exact(cot, owned.astype(jnp.float32), ALONG)
    is_value = iota(kept.shape, 0) < objectives
    row_dot = jnp.sum(jnp.where(is_value, kept * own_cot, 0.0), axis=0, keepdims=True)
    weight = kept[objectives : objectives + 1]
    beta = kept[objectives + 1 : objectives + 2] * row_dot
    both = jnp.concatenate([weight, beta, jnp.zeros((LANES - 2, tokens), jnp.float32)], axis=0)
    columns = both.T
    member = owned.astype(jnp.bfloat16)
    directions = jnp.concatenate(in_three(gain * direction), axis=0)
    own = dot32(jnp.concatenate([member] * 3, axis=0), directions, FIRST)
    grad = columns[:, 0:1] * own - columns[:, 1:2] * visual_ref[...].astype(jnp.float32)
    visual_grad_ref[...] = grad.astype(jnp.bfloat16)


def whole(count):
    return [pl.BlockSpec(memory_space=pltpu.VMEM)] * count


def in_hbm(array):
    return pltpu.with_memory_space_constraint(array, pltpu.HBM)


def scalars(count):
    return [pl.BlockSpec(memory_space=pltpu.SMEM)] * count


def folded(parts, copies, kind, name):
    return pl.pallas_call(
        fold_kernel,
        out_shape=jax.ShapeDtypeStruct((copies, *parts.shape[1:]), kind),
        in_specs=whole(1),
        out_specs=pl.BlockSpec(memory_space=pltpu.VMEM),
        compiler_params=VMEM,
        name=f"fold_{name}",
    )(parts)


def on_device(
    hidden, merge_weight, text_embed, gain, head_weight, owner, vis_row, lengths, labels, targets
):
    groups, near = lax.axis_size(GRP), lax.axis_size(NEAR)
    tokens, depth = hidden.shape
    positions, width = text_embed.shape
    objectives = head_weight.shape[1]
    cap = vis_row.shape[1] // groups
    features = float(width * lax.axis_size(TP))
    scale = float(positions * groups // 16)
    me = lax.axis_index(GRP).astype(jnp.int32).reshape(1)
    owners = owner.reshape(1, tokens)
    gain_row = gain.reshape(1, width)
    head = head_weight.T
    marks = labels.T

    flags = pl.pallas_call(
        functools.partial(flags_kernel, cap),
        out_shape=jax.ShapeDtypeStruct((groups, LANES), jnp.float32),
        in_specs=scalars(1) + whole(3),
        out_specs=pl.BlockSpec(memory_space=pltpu.VMEM),
        compiler_params=VMEM,
        name="flags",
    )(lengths, in_hbm(owners), in_hbm(vis_row), in_hbm(targets))
    told = lax.all_to_all(
        flags.reshape(groups // near, near, LANES), "far", split_axis=0, concat_axis=0, tiled=True
    )

    chunks = 5
    rows = tokens + positions
    visual, stats = pl.pallas_call(
        stats_kernel,
        out_shape=(
            jax.ShapeDtypeStruct((tokens, width), jnp.bfloat16),
            jax.ShapeDtypeStruct((8, 2 * rows + tight_lanes(rows)), jnp.float32),
        ),
        in_specs=[pl.BlockSpec(memory_space=pl.ANY)]
        + [pl.BlockSpec(memory_space=pltpu.HBM)] * 3
        + whole(2),
        out_specs=tuple(whole(2)),
        scratch_shapes=[
            pltpu.VMEM((chunks, tokens, depth // chunks), jnp.bfloat16),
            pltpu.VMEM((chunks, depth // chunks, width), jnp.bfloat16),
            pltpu.VMEM((positions, width), jnp.bfloat16),
            pltpu.VMEM((K_ROWS, width), jnp.float32),
            pltpu.SemaphoreType.DMA((2 * chunks + 1,)),
        ],
        compiler_params=VMEM,
        name="stats",
    )(flags, in_hbm(hidden), in_hbm(merge_weight), in_hbm(text_embed), in_hbm(gain_row), in_hbm(head))
    stats, told = lax.optimization_barrier((stats, told))
    told = lax.all_to_all(told, NEAR, split_axis=1, concat_axis=1, tiled=True)
    told = told.reshape(groups, LANES)
    stats = lax.all_gather(jnp.sum(lax.all_gather(stats, "tx"), axis=0), "ty")

    pooled, kept = pl.pallas_call(
        functools.partial(pooled_kernel, cap, objectives, features),
        out_shape=(
            jax.ShapeDtypeStruct((groups, width + LANES), jnp.float32),
            jax.ShapeDtypeStruct((K_ROWS, tokens), jnp.float32),
        ),
        in_specs=scalars(2) + whole(6),
        out_specs=tuple(whole(2)),
        compiler_params=VMEM,
        name="pooled",
    )(me, lengths, stats, told, owners, vis_row, visual, text_embed)
    block = pooled.reshape(near, groups // near, width + LANES)
    block = lax.all_to_all(block, NEAR, split_axis=0, concat_axis=0, tiled=True)
    block = folded(block, lax.axis_size("far"), jnp.bfloat16, "near")
    block = lax.all_to_all(block, "far", split_axis=0, concat_axis=0, tiled=True)
    block = folded(block, near, jnp.float32, "far")
    block = lax.all_to_all(block, NEAR, split_axis=0, concat_axis=0, tiled=True)
    pooled = block.reshape(groups, width + LANES)

    reward, visual_grad, head_grad, gain_grad = pl.pallas_call(
        functools.partial(grads_kernel, cap, scale),
        out_shape=(
            jax.ShapeDtypeStruct((1, LANES), jnp.float32),
            jax.ShapeDtypeStruct((tokens, width), jnp.bfloat16),
            jax.ShapeDtypeStruct((objectives, width), jnp.float32),
            jax.ShapeDtypeStruct((1, width), jnp.float32),
        ),
        in_specs=scalars(1) + whole(8),
        out_specs=tuple(whole(4)),
        scratch_shapes=[
            pltpu.VMEM((K_ROWS, groups), jnp.int32),
            pltpu.VMEM((K_ROWS, width), jnp.float32),
        ],
        compiler_params=VMEM,
        name="grads",
    )(me, pooled, kept, told, owners, visual, marks, gain_row, head)
    return reward[:, :objectives], visual_grad, head_grad.T, gain_grad.reshape(width)


def solution(mesh):
    groups, tp = mesh.shape["grp"], mesh.shape["tp"]
    near = 4 if groups % 16 == 0 else 2
    ty = 4 if tp % 16 == 0 else 1
    torus = Mesh(
        mesh.devices.reshape(groups // (2 * near), near, 2, ty, tp // ty),
        ("far", "near", "core", "ty", "tx"),
    )
    placed = (
        P(GRP, None),
        P(None, TP),
        P(GRP, TP),
        P(TP),
        P(TP, None),
        P(GRP, None),
        P(GRP, None),
        P(GRP),
        P(),
        P(GRP, None),
    )
    return jax.shard_map(
        on_device,
        mesh=torus,
        in_specs=placed,
        out_specs=(P(GRP, None), P(GRP, TP), P(TP, None), P(TP)),
        check_vma=False,
    )
```

```python
import functools

import jax
import jax.numpy as jnp
from jax import lax
from jax.experimental import pallas as pl
from jax.experimental.pallas import tpu as pltpu
from jax.sharding import Mesh
from jax.sharding import PartitionSpec as P

GRP = ("far", "near", "core")
NEAR = ("near", "core")
TP = ("ty", "tx")
EPSILON = 1e-06
LANES = 128
K_ROWS = 24
SIDE = 32
VMEM = pltpu.CompilerParams(vmem_limit_bytes=48 * 2**20)
EXACT = lax.Precision.HIGHEST
LAST = (((1,), (1,)), ((), ()))
FIRST = (((0,), (0,)), ((), ()))
ALONG = (((1,), (0,)), ((), ()))


def iota(shape, dim):
    return lax.broadcasted_iota(jnp.int32, shape, dim)


def in_three(x):
    hi = x.astype(jnp.bfloat16)
    rest = x - hi.astype(jnp.float32)
    mid = rest.astype(jnp.bfloat16)
    return hi, mid, (rest - mid.astype(jnp.float32)).astype(jnp.bfloat16)


def dot32(a, b, dims):
    return lax.dot_general(a, b, dims, preferred_element_type=jnp.float32)


def dot_exact(a, b, dims):
    return lax.dot_general(a, b, dims, precision=EXACT, preferred_element_type=jnp.float32)


def target_lane(cap):
    return -(-(cap + 2) // 8) * 8


def packed(pooled, reward):
    terms = [term.astype(jnp.float32) for term in in_three(reward)]
    terms.append(jnp.zeros((reward.shape[0], LANES - 3 * SIDE), jnp.float32))
    side = jnp.concatenate(terms, axis=1)
    return jnp.concatenate([pooled, side], axis=1).astype(jnp.bfloat16)


def rewards_of(side):
    return side[:, :SIDE] + side[:, SIDE : 2 * SIDE] + side[:, 2 * SIDE : 3 * SIDE]


def padded(ref, scratch):
    scratch[...] = jnp.zeros_like(scratch)
    scratch[: ref.shape[0]] = ref[...]
    return scratch[...]


def tight_lanes(rows):
    return -(-rows // (2 * LANES)) * LANES


def tight(stats):
    rows = stats.shape[1]
    half = tight_lanes(rows)
    last = jnp.concatenate([stats[16:20, :half], stats[16:20, rows - half :]], axis=0)
    return jnp.concatenate([stats[:8], stats[8:16], last], axis=1)


def loose(packed_stats, rows):
    half = tight_lanes(rows)
    last = packed_stats[:, 2 * rows :]
    last = jnp.concatenate([last[:4, :half], last[4:, 2 * half - rows :]], axis=1)
    last = jnp.concatenate([last, jnp.zeros_like(last)], axis=0)
    return jnp.concatenate([packed_stats[:, :rows], packed_stats[:, rows : 2 * rows], last], axis=0)


def flags_kernel(cap, length_ref, owner_ref, rows_ref, targets_ref, out_ref):
    groups = out_ref.shape[0]
    slots = rows_ref.shape[1]
    length = length_ref[0]
    live = (rows_ref[...] < length).astype(jnp.float32)
    slot = iota((groups, slots), 1)
    first = iota((groups, slots), 0) * cap
    mine = jnp.where((slot >= first) & (slot < first + cap), live, 0.0).astype(jnp.bfloat16)
    rank = lax.rem(iota((LANES, slots), 1), cap)
    place = (rank == iota((LANES, slots), 0)).astype(jnp.bfloat16)
    flags = dot32(mine, place, LAST)
    owned = (owner_ref[...] == iota((groups, owner_ref.shape[1]), 0)).astype(jnp.float32)
    count = jnp.sum(owned, axis=1, keepdims=True)
    lane = iota((groups, LANES), 1)
    flags = jnp.where(lane == cap, count, flags)
    out_ref[...] = jnp.where(lane == cap + 1, length.astype(jnp.float32), flags)
    first = target_lane(cap)
    objectives = targets_ref.shape[1]
    out_ref[:, first : first + objectives] = jnp.broadcast_to(
        targets_ref[...], (groups, objectives)
    )


def stats_kernel(
    after_ref,
    hidden_ref,
    weight_ref,
    text_ref,
    gain_ref,
    head_ref,
    visual_ref,
    stats_ref,
    hidden,
    weight,
    text,
    head,
    arrived,
):
    chunks, tokens, depth = hidden.shape
    objectives = head_ref.shape[0]
    copies = [pltpu.make_async_copy(text_ref, text, arrived.at[0])]
    for i in range(chunks):
        part = pl.ds(i * depth, depth)
        copies.append(
            pltpu.make_async_copy(hidden_ref.at[:, part], hidden.at[i], arrived.at[2 * i + 1])
        )
        copies.append(
            pltpu.make_async_copy(weight_ref.at[part, :], weight.at[i], arrived.at[2 * i + 2])
        )
    for copy in copies:
        copy.start()
    gained = jnp.concatenate(in_three(gain_ref[...] * padded(head_ref, head)), axis=0)

    def of_rows(x):
        parts = dot32(gained, x, LAST)
        value = parts[:K_ROWS] + parts[K_ROWS : 2 * K_ROWS] + parts[2 * K_ROWS :]
        wide = x.astype(jnp.float32)
        square = wide * wide
        lanes = square[:, :LANES]
        for at in range(LANES, x.shape[1], LANES):
            lanes = lanes + square[:, at : at + LANES]
        terms = jnp.concatenate(in_three(lanes), axis=1)
        squares = dot32(jnp.ones((K_ROWS, terms.shape[1]), jnp.bfloat16), terms, LAST)
        return jnp.where(iota(value.shape, 0) == objectives, squares, value)

    copies[0].wait()
    of_text = of_rows(text[...])
    total = None
    for i in range(chunks):
        copies[2 * i + 1].wait()
        copies[2 * i + 2].wait()
        part = dot32(hidden[i], weight[i], ALONG)
        total = part if total is None else total + part
    visual = total.astype(jnp.bfloat16)
    visual_ref[...] = visual
    stats_ref[...] = tight(jnp.concatenate([of_rows(visual), of_text], axis=1))


def pooled_kernel(
    cap,
    objectives,
    features,
    me_ref,
    length_ref,
    stats_ref,
    flags_ref,
    owner_ref,
    rows_ref,
    visual_ref,
    text_ref,
    pooled_ref,
    kept_ref,
):
    tokens, width = visual_ref.shape
    positions = text_ref.shape[0]
    groups = flags_ref.shape[0]
    slots = rows_ref.shape[1]
    stats = stats_ref[0]
    for part in range(1, stats_ref.shape[0]):
        stats = stats + stats_ref[part]
    stats = loose(stats, tokens + positions)
    inv = lax.rsqrt(stats[objectives : objectives + 1] / features + EPSILON)
    flags = flags_ref[...]

    owned = owner_ref[...] == iota((groups, tokens), 0)
    member = owned.astype(jnp.bfloat16)
    before = (iota((tokens, tokens), 0) < iota((tokens, tokens), 1)).astype(jnp.bfloat16)
    earlier = dot32(member, before, ALONG)
    rank = jnp.sum(jnp.where(owned, earlier, 0.0), axis=0, keepdims=True)
    told = dot_exact(flags, owned.astype(jnp.float32), FIRST)
    at = iota(told.shape, 0)
    live = jnp.sum(
        jnp.where((at < cap) & (at == rank.astype(jnp.int32)), told, 0.0), axis=0, keepdims=True
    )
    token_inv = inv[:, :tokens]
    token_weight = live * token_inv / told[cap + 1 : cap + 2]

    length = length_ref[0]
    slot = iota((groups, slots), 1)
    first = iota((groups, slots), 0) * cap
    count = flags[:, cap : cap + 1].astype(jnp.int32)
    used = jnp.sum(((slot >= first) & (slot < first + count)).astype(jnp.float32), axis=0, keepdims=True)
    row = rows_ref[...]
    tall = positions // LANES
    high = jnp.where(lax.div(row, LANES) == iota((tall, slots), 0), used, 0.0).astype(jnp.bfloat16)
    low = (lax.rem(row, LANES) == iota((LANES, slots), 0)).astype(jnp.bfloat16)
    replaced = dot32(high, low, LAST)
    replaced = jnp.concatenate([replaced[i : i + 1] for i in range(tall)], axis=1)
    stays = (iota((1, positions), 1) < length) & (replaced < 0.5)
    text_weight = jnp.where(stays, inv[:, tokens:], 0.0) / length.astype(jnp.float32)

    spread = jnp.where(owned, token_weight, 0.0)
    three = dot32(jnp.concatenate(in_three(spread), axis=0), visual_ref[...], ALONG)
    pooled = three[:groups] + three[groups : 2 * groups] + three[2 * groups :]
    reward = dot_exact(spread, stats[:, :tokens], LAST)
    split = jnp.concatenate(in_three(jnp.broadcast_to(text_weight, (16, positions))), axis=0)
    text_three = dot32(split, text_ref[...], ALONG)
    text_pooled = text_three[0:1] + text_three[16:17] + text_three[32:33]
    text_reward = dot_exact(
        jnp.broadcast_to(text_weight, (8, positions)), stats[:, tokens:], LAST
    )[0:1]
    mine = iota((groups, 1), 0) == me_ref[0]
    pooled_ref[:, :width] = pooled + jnp.where(mine, text_pooled, 0.0)
    reward = reward + jnp.where(mine, text_reward, 0.0)
    pooled_ref[:, width:] = jnp.zeros((groups, LANES), jnp.float32)
    pooled_ref[:, width : width + objectives] = reward[:, :objectives]
    kept = jnp.where(iota((K_ROWS, tokens), 0) == objectives, token_weight, stats[:, :tokens])
    factor = token_weight * token_inv * token_inv / features
    kept_ref[...] = jnp.where(iota((K_ROWS, tokens), 0) == objectives + 1, factor, kept)


def fold_kernel(parts_ref, out_ref):
    total = parts_ref[0].astype(jnp.float32)
    for part in range(1, parts_ref.shape[0]):
        total = total + parts_ref[part].astype(jnp.float32)
    width = total.shape[1] - LANES
    joined, side = total[:, :width], total[:, width:]
    if out_ref.dtype == jnp.bfloat16:
        once = packed(joined, side[:, :SIDE])
    else:
        spare = jnp.zeros((side.shape[0], LANES - SIDE), jnp.float32)
        once = jnp.concatenate([joined, rewards_of(side), spare], axis=1)
    for copy in range(out_ref.shape[0]):
        out_ref[copy] = once


def grads_kernel(
    cap,
    scale,
    me_ref,
    pooled_ref,
    kept_ref,
    flags_ref,
    owner_ref,
    visual_ref,
    labels_ref,
    gain_ref,
    head_ref,
    reward_ref,
    visual_grad_ref,
    head_grad_ref,
    gain_grad_ref,
    marks,
    head_all,
):
    tokens, width = visual_ref.shape
    groups = flags_ref.shape[0]
    objectives = labels_ref.shape[0]
    z = pooled_ref[:, :width]
    rest = pooled_ref[:, width:]
    mine = iota(rest.shape, 0) == me_ref[0]
    reward_ref[...] = jnp.sum(jnp.where(mine, rest, 0.0), axis=0, keepdims=True)
    first = target_lane(cap)
    error = rest.T[:K_ROWS] - flags_ref[...].T[first : first + K_ROWS]
    labels = padded(labels_ref, marks).astype(jnp.float32)
    count = jnp.maximum(jnp.sum(labels, axis=1, keepdims=True), 1.0)
    cot = scale * labels * error / count
    gain = gain_ref[...]
    head = padded(head_ref, head_all)
    head_grad_ref[...] = (gain * dot_exact(cot, z, ALONG))[:objectives]
    direction = dot_exact(cot, head, FIRST)
    gain_grad_ref[...] = jnp.sum(z * direction, axis=0, keepdims=True)
    owned = owner_ref[...] == iota((groups, tokens), 0)
    kept = kept_ref[...]
    own_cot = dot_exact(cot, owned.astype(jnp.float32), ALONG)
    is_value = iota(kept.shape, 0) < objectives
    row_dot = jnp.sum(jnp.where(is_value, kept * own_cot, 0.0), axis=0, keepdims=True)
    weight = kept[objectives : objectives + 1]
    beta = kept[objectives + 1 : objectives + 2] * row_dot
    both = jnp.concatenate([weight, beta, jnp.zeros((LANES - 2, tokens), jnp.float32)], axis=0)
    columns = both.T
    member = owned.astype(jnp.bfloat16)
    directions = jnp.concatenate(in_three(gain * direction), axis=0)
    own = dot32(jnp.concatenate([member] * 3, axis=0), directions, FIRST)
    grad = columns[:, 0:1] * own - columns[:, 1:2] * visual_ref[...].astype(jnp.float32)
    visual_grad_ref[...] = grad.astype(jnp.bfloat16)


def whole(count):
    return [pl.BlockSpec(memory_space=pltpu.VMEM)] * count


def in_hbm(array):
    return pltpu.with_memory_space_constraint(array, pltpu.HBM)


def scalars(count):
    return [pl.BlockSpec(memory_space=pltpu.SMEM)] * count


def folded(parts, copies, kind, name):
    return pl.pallas_call(
        fold_kernel,
        out_shape=jax.ShapeDtypeStruct((copies, *parts.shape[1:]), kind),
        in_specs=whole(1),
        out_specs=pl.BlockSpec(memory_space=pltpu.VMEM),
        compiler_params=VMEM,
        name=f"fold_{name}",
    )(parts)


def on_device(
    hidden, merge_weight, text_embed, gain, head_weight, owner, vis_row, lengths, labels, targets
):
    groups, near = lax.axis_size(GRP), lax.axis_size(NEAR)
    tokens, depth = hidden.shape
    positions, width = text_embed.shape
    objectives = head_weight.shape[1]
    cap = vis_row.shape[1] // groups
    features = float(width * lax.axis_size(TP))
    scale = float(positions * groups // 16)
    me = lax.axis_index(GRP).astype(jnp.int32).reshape(1)
    owners = owner.reshape(1, tokens)
    gain_row = gain.reshape(1, width)
    head = head_weight.T
    marks = labels.T

    flags = pl.pallas_call(
        functools.partial(flags_kernel, cap),
        out_shape=jax.ShapeDtypeStruct((groups, LANES), jnp.float32),
        in_specs=scalars(1) + whole(3),
        out_specs=pl.BlockSpec(memory_space=pltpu.VMEM),
        compiler_params=VMEM,
        name="flags",
    )(lengths, in_hbm(owners), in_hbm(vis_row), in_hbm(targets))
    told = lax.all_to_all(
        flags.reshape(groups, 1, LANES), GRP, split_axis=0, concat_axis=0, tiled=True
    ).reshape(groups, LANES)

    chunks = 5
    rows = tokens + positions
    visual, stats = pl.pallas_call(
        stats_kernel,
        out_shape=(
            jax.ShapeDtypeStruct((tokens, width), jnp.bfloat16),
            jax.ShapeDtypeStruct((8, 2 * rows + tight_lanes(rows)), jnp.float32),
        ),
        in_specs=[pl.BlockSpec(memory_space=pl.ANY)]
        + [pl.BlockSpec(memory_space=pltpu.HBM)] * 3
        + whole(2),
        out_specs=tuple(whole(2)),
        scratch_shapes=[
            pltpu.VMEM((chunks, tokens, depth // chunks), jnp.bfloat16),
            pltpu.VMEM((chunks, depth // chunks, width), jnp.bfloat16),
            pltpu.VMEM((positions, width), jnp.bfloat16),
            pltpu.VMEM((K_ROWS, width), jnp.float32),
            pltpu.SemaphoreType.DMA((2 * chunks + 1,)),
        ],
        compiler_params=VMEM,
        name="stats",
    )(flags, in_hbm(hidden), in_hbm(merge_weight), in_hbm(text_embed), in_hbm(gain_row), in_hbm(head))
    stats = lax.all_gather(jnp.sum(lax.all_gather(stats, "tx"), axis=0), "ty")

    pooled, kept = pl.pallas_call(
        functools.partial(pooled_kernel, cap, objectives, features),
        out_shape=(
            jax.ShapeDtypeStruct((groups, width + LANES), jnp.float32),
            jax.ShapeDtypeStruct((K_ROWS, tokens), jnp.float32),
        ),
        in_specs=scalars(2) + whole(6),
        out_specs=tuple(whole(2)),
        compiler_params=VMEM,
        name="pooled",
    )(me, lengths, stats, told, owners, vis_row, visual, text_embed)
    block = pooled.reshape(near, groups // near, width + LANES)
    block = lax.all_to_all(block, NEAR, split_axis=0, concat_axis=0, tiled=True)
    block = folded(block, lax.axis_size("far"), jnp.bfloat16, "near")
    block = lax.all_to_all(block, "far", split_axis=0, concat_axis=0, tiled=True)
    block = folded(block, near, jnp.float32, "far")
    block = lax.all_to_all(block, NEAR, split_axis=0, concat_axis=0, tiled=True)
    pooled = block.reshape(groups, width + LANES)

    reward, visual_grad, head_grad, gain_grad = pl.pallas_call(
        functools.partial(grads_kernel, cap, scale),
        out_shape=(
            jax.ShapeDtypeStruct((1, LANES), jnp.float32),
            jax.ShapeDtypeStruct((tokens, width), jnp.bfloat16),
            jax.ShapeDtypeStruct((objectives, width), jnp.float32),
            jax.ShapeDtypeStruct((1, width), jnp.float32),
        ),
        in_specs=scalars(1) + whole(8),
        out_specs=tuple(whole(4)),
        scratch_shapes=[
            pltpu.VMEM((K_ROWS, groups), jnp.int32),
            pltpu.VMEM((K_ROWS, width), jnp.float32),
        ],
        compiler_params=VMEM,
        name="grads",
    )(me, pooled, kept, told, owners, visual, marks, gain_row, head)
    return reward[:, :objectives], visual_grad, head_grad.T, gain_grad.reshape(width)


def solution(mesh):
    groups, tp = mesh.shape["grp"], mesh.shape["tp"]
    near = 8 if groups % 32 == 0 else 2
    ty = 4 if tp % 16 == 0 else 1
    torus = Mesh(
        mesh.devices.reshape(groups // (2 * near), near, 2, ty, tp // ty),
        ("far", "near", "core", "ty", "tx"),
    )
    placed = (
        P(GRP, None),
        P(None, TP),
        P(GRP, TP),
        P(TP),
        P(TP, None),
        P(GRP, None),
        P(GRP, None),
        P(GRP),
        P(),
        P(GRP, None),
    )
    return jax.shard_map(
        on_device,
        mesh=torus,
        in_specs=placed,
        out_specs=(P(GRP, None), P(GRP, TP), P(TP, None), P(TP)),
        check_vma=False,
    )
```

```python
import functools

import jax
import jax.numpy as jnp
from jax import lax
from jax.experimental import pallas as pl
from jax.experimental.pallas import tpu as pltpu
from jax.sharding import Mesh
from jax.sharding import PartitionSpec as P

GRP = ("far", "near", "core")
NEAR = ("near", "core")
TP = ("ty", "tx")
EPSILON = 1e-06
LANES = 128
K_ROWS = 24
SIDE = 32
VMEM = pltpu.CompilerParams(vmem_limit_bytes=48 * 2**20)
EXACT = lax.Precision.HIGHEST
LAST = (((1,), (1,)), ((), ()))
FIRST = (((0,), (0,)), ((), ()))
ALONG = (((1,), (0,)), ((), ()))


def iota(shape, dim):
    return lax.broadcasted_iota(jnp.int32, shape, dim)


def in_three(x):
    hi = x.astype(jnp.bfloat16)
    rest = x - hi.astype(jnp.float32)
    mid = rest.astype(jnp.bfloat16)
    return hi, mid, (rest - mid.astype(jnp.float32)).astype(jnp.bfloat16)


def dot32(a, b, dims):
    return lax.dot_general(a, b, dims, preferred_element_type=jnp.float32)


def dot_exact(a, b, dims):
    return lax.dot_general(a, b, dims, precision=EXACT, preferred_element_type=jnp.float32)


def target_lane(cap):
    return -(-(cap + 2) // 8) * 8


def packed(pooled, reward):
    terms = [term.astype(jnp.float32) for term in in_three(reward)]
    terms.append(jnp.zeros((reward.shape[0], LANES - 3 * SIDE), jnp.float32))
    side = jnp.concatenate(terms, axis=1)
    return jnp.concatenate([pooled, side], axis=1).astype(jnp.bfloat16)


def rewards_of(side):
    return side[:, :SIDE] + side[:, SIDE : 2 * SIDE] + side[:, 2 * SIDE : 3 * SIDE]


def padded(ref, scratch):
    scratch[...] = jnp.zeros_like(scratch)
    scratch[: ref.shape[0]] = ref[...]
    return scratch[...]


def tight_lanes(rows):
    return -(-rows // (2 * LANES)) * LANES


def tight(stats):
    rows = stats.shape[1]
    half = tight_lanes(rows)
    last = jnp.concatenate([stats[16:20, :half], stats[16:20, rows - half :]], axis=0)
    return jnp.concatenate([stats[:8], stats[8:16], last], axis=1)


def loose(packed_stats, rows):
    half = tight_lanes(rows)
    last = packed_stats[:, 2 * rows :]
    last = jnp.concatenate([last[:4, :half], last[4:, 2 * half - rows :]], axis=1)
    last = jnp.concatenate([last, jnp.zeros_like(last)], axis=0)
    return jnp.concatenate([packed_stats[:, :rows], packed_stats[:, rows : 2 * rows], last], axis=0)


def fetched(sources, targets, arrived):
    copies = []
    for i, (source, target) in enumerate(zip(sources, targets)):
        copies.append(pltpu.make_async_copy(source, target, arrived.at[i]))
    for copy in copies:
        copy.start()
    return copies


def flags_kernel(
    cap,
    length_ref,
    owner_hbm,
    rows_hbm,
    targets_hbm,
    out_ref,
    owner_ref,
    rows_ref,
    targets_ref,
    arrived,
):
    copies = fetched(
        (owner_hbm, rows_hbm, targets_hbm), (owner_ref, rows_ref, targets_ref), arrived
    )
    for copy in copies:
        copy.wait()
    groups = out_ref.shape[0]
    slots = rows_ref.shape[1]
    length = length_ref[0]
    live = (rows_ref[...] < length).astype(jnp.float32)
    slot = iota((groups, slots), 1)
    first = iota((groups, slots), 0) * cap
    mine = jnp.where((slot >= first) & (slot < first + cap), live, 0.0).astype(jnp.bfloat16)
    rank = lax.rem(iota((LANES, slots), 1), cap)
    place = (rank == iota((LANES, slots), 0)).astype(jnp.bfloat16)
    flags = dot32(mine, place, LAST)
    owned = (owner_ref[...] == iota((groups, owner_ref.shape[1]), 0)).astype(jnp.float32)
    count = jnp.sum(owned, axis=1, keepdims=True)
    lane = iota((groups, LANES), 1)
    flags = jnp.where(lane == cap, count, flags)
    out_ref[...] = jnp.where(lane == cap + 1, length.astype(jnp.float32), flags)
    first = target_lane(cap)
    objectives = targets_ref.shape[1]
    out_ref[:, first : first + objectives] = jnp.broadcast_to(
        targets_ref[...], (groups, objectives)
    )


def stats_kernel(
    after_ref,
    hidden_ref,
    weight_ref,
    text_ref,
    gain_hbm,
    head_hbm,
    visual_ref,
    stats_ref,
    hidden,
    weight,
    text,
    head,
    gain_ref,
    head_ref,
    arrived,
    small_arrived,
):
    chunks, tokens, depth = hidden.shape
    objectives = head_ref.shape[0]
    small = fetched((gain_hbm, head_hbm), (gain_ref, head_ref), small_arrived)
    copies = [pltpu.make_async_copy(text_ref, text, arrived.at[0])]
    for i in range(chunks):
        part = pl.ds(i * depth, depth)
        copies.append(
            pltpu.make_async_copy(hidden_ref.at[:, part], hidden.at[i], arrived.at[2 * i + 1])
        )
        copies.append(
            pltpu.make_async_copy(weight_ref.at[part, :], weight.at[i], arrived.at[2 * i + 2])
        )
    for copy in copies:
        copy.start()
    for copy in small:
        copy.wait()
    gained = jnp.concatenate(in_three(gain_ref[...] * padded(head_ref, head)), axis=0)

    def of_rows(x):
        parts = dot32(gained, x, LAST)
        value = parts[:K_ROWS] + parts[K_ROWS : 2 * K_ROWS] + parts[2 * K_ROWS :]
        wide = x.astype(jnp.float32)
        square = wide * wide
        lanes = square[:, :LANES]
        for at in range(LANES, x.shape[1], LANES):
            lanes = lanes + square[:, at : at + LANES]
        terms = jnp.concatenate(in_three(lanes), axis=1)
        squares = dot32(jnp.ones((K_ROWS, terms.shape[1]), jnp.bfloat16), terms, LAST)
        return jnp.where(iota(value.shape, 0) == objectives, squares, value)

    copies[0].wait()
    of_text = of_rows(text[...])
    total = None
    for i in range(chunks):
        copies[2 * i + 1].wait()
        copies[2 * i + 2].wait()
        part = dot32(hidden[i], weight[i], ALONG)
        total = part if total is None else total + part
    visual = total.astype(jnp.bfloat16)
    visual_ref[...] = visual
    stats_ref[...] = tight(jnp.concatenate([of_rows(visual), of_text], axis=1))


def pooled_kernel(
    cap,
    objectives,
    features,
    me_ref,
    length_ref,
    stats_ref,
    flags_ref,
    owner_ref,
    rows_ref,
    visual_ref,
    text_ref,
    pooled_ref,
    kept_ref,
):
    tokens, width = visual_ref.shape
    positions = text_ref.shape[0]
    groups = flags_ref.shape[0]
    slots = rows_ref.shape[1]
    stats = stats_ref[0]
    for part in range(1, stats_ref.shape[0]):
        stats = stats + stats_ref[part]
    stats = loose(stats, tokens + positions)
    inv = lax.rsqrt(stats[objectives : objectives + 1] / features + EPSILON)
    flags = flags_ref[...]

    owned = owner_ref[...] == iota((groups, tokens), 0)
    member = owned.astype(jnp.bfloat16)
    before = (iota((tokens, tokens), 0) < iota((tokens, tokens), 1)).astype(jnp.bfloat16)
    earlier = dot32(member, before, ALONG)
    rank = jnp.sum(jnp.where(owned, earlier, 0.0), axis=0, keepdims=True)
    told = dot_exact(flags, owned.astype(jnp.float32), FIRST)
    at = iota(told.shape, 0)
    live = jnp.sum(
        jnp.where((at < cap) & (at == rank.astype(jnp.int32)), told, 0.0), axis=0, keepdims=True
    )
    token_inv = inv[:, :tokens]
    token_weight = live * token_inv / told[cap + 1 : cap + 2]

    length = length_ref[0]
    slot = iota((groups, slots), 1)
    first = iota((groups, slots), 0) * cap
    count = flags[:, cap : cap + 1].astype(jnp.int32)
    used = jnp.sum(((slot >= first) & (slot < first + count)).astype(jnp.float32), axis=0, keepdims=True)
    row = rows_ref[...]
    tall = positions // LANES
    high = jnp.where(lax.div(row, LANES) == iota((tall, slots), 0), used, 0.0).astype(jnp.bfloat16)
    low = (lax.rem(row, LANES) == iota((LANES, slots), 0)).astype(jnp.bfloat16)
    replaced = dot32(high, low, LAST)
    replaced = jnp.concatenate([replaced[i : i + 1] for i in range(tall)], axis=1)
    stays = (iota((1, positions), 1) < length) & (replaced < 0.5)
    text_weight = jnp.where(stays, inv[:, tokens:], 0.0) / length.astype(jnp.float32)

    spread = jnp.where(owned, token_weight, 0.0)
    three = dot32(jnp.concatenate(in_three(spread), axis=0), visual_ref[...], ALONG)
    pooled = three[:groups] + three[groups : 2 * groups] + three[2 * groups :]
    reward = dot_exact(spread, stats[:, :tokens], LAST)
    split = jnp.concatenate(in_three(jnp.broadcast_to(text_weight, (16, positions))), axis=0)
    text_three = dot32(split, text_ref[...], ALONG)
    text_pooled = text_three[0:1] + text_three[16:17] + text_three[32:33]
    text_reward = dot_exact(
        jnp.broadcast_to(text_weight, (8, positions)), stats[:, tokens:], LAST
    )[0:1]
    mine = iota((groups, 1), 0) == me_ref[0]
    pooled_ref[:, :width] = pooled + jnp.where(mine, text_pooled, 0.0)
    reward = reward + jnp.where(mine, text_reward, 0.0)
    pooled_ref[:, width:] = jnp.zeros((groups, LANES), jnp.float32)
    pooled_ref[:, width : width + objectives] = reward[:, :objectives]
    kept = jnp.where(iota((K_ROWS, tokens), 0) == objectives, token_weight, stats[:, :tokens])
    factor = token_weight * token_inv * token_inv / features
    kept_ref[...] = jnp.where(iota((K_ROWS, tokens), 0) == objectives + 1, factor, kept)


def fold_kernel(parts_ref, out_ref):
    total = parts_ref[0].astype(jnp.float32)
    for part in range(1, parts_ref.shape[0]):
        total = total + parts_ref[part].astype(jnp.float32)
    width = total.shape[1] - LANES
    joined, side = total[:, :width], total[:, width:]
    if out_ref.dtype == jnp.bfloat16:
        once = packed(joined, side[:, :SIDE])
    else:
        spare = jnp.zeros((side.shape[0], LANES - SIDE), jnp.float32)
        once = jnp.concatenate([joined, rewards_of(side), spare], axis=1)
    for copy in range(out_ref.shape[0]):
        out_ref[copy] = once


def grads_kernel(
    cap,
    scale,
    me_ref,
    pooled_ref,
    kept_ref,
    flags_ref,
    owner_ref,
    visual_ref,
    labels_ref,
    gain_ref,
    head_ref,
    reward_ref,
    visual_grad_ref,
    head_grad_ref,
    gain_grad_ref,
    marks,
    head_all,
):
    tokens, width = visual_ref.shape
    groups = flags_ref.shape[0]
    objectives = labels_ref.shape[0]
    z = pooled_ref[:, :width]
    rest = pooled_ref[:, width:]
    mine = iota(rest.shape, 0) == me_ref[0]
    reward_ref[...] = jnp.sum(jnp.where(mine, rest, 0.0), axis=0, keepdims=True)
    first = target_lane(cap)
    error = rest.T[:K_ROWS] - flags_ref[...].T[first : first + K_ROWS]
    labels = padded(labels_ref, marks).astype(jnp.float32)
    count = jnp.maximum(jnp.sum(labels, axis=1, keepdims=True), 1.0)
    cot = scale * labels * error / count
    gain = gain_ref[...]
    head = padded(head_ref, head_all)
    head_grad_ref[...] = (gain * dot_exact(cot, z, ALONG))[:objectives]
    direction = dot_exact(cot, head, FIRST)
    gain_grad_ref[...] = jnp.sum(z * direction, axis=0, keepdims=True)
    owned = owner_ref[...] == iota((groups, tokens), 0)
    kept = kept_ref[...]
    own_cot = dot_exact(cot, owned.astype(jnp.float32), ALONG)
    is_value = iota(kept.shape, 0) < objectives
    row_dot = jnp.sum(jnp.where(is_value, kept * own_cot, 0.0), axis=0, keepdims=True)
    weight = kept[objectives : objectives + 1]
    beta = kept[objectives + 1 : objectives + 2] * row_dot
    both = jnp.concatenate([weight, beta, jnp.zeros((LANES - 2, tokens), jnp.float32)], axis=0)
    columns = both.T
    member = owned.astype(jnp.bfloat16)
    directions = jnp.concatenate(in_three(gain * direction), axis=0)
    own = dot32(jnp.concatenate([member] * 3, axis=0), directions, FIRST)
    grad = columns[:, 0:1] * own - columns[:, 1:2] * visual_ref[...].astype(jnp.float32)
    visual_grad_ref[...] = grad.astype(jnp.bfloat16)


def whole(count):
    return [pl.BlockSpec(memory_space=pltpu.VMEM)] * count


def in_hbm(array):
    return pltpu.with_memory_space_constraint(array, pltpu.HBM)


def scalars(count):
    return [pl.BlockSpec(memory_space=pltpu.SMEM)] * count


def folded(parts, copies, kind, name):
    return pl.pallas_call(
        fold_kernel,
        out_shape=jax.ShapeDtypeStruct((copies, *parts.shape[1:]), kind),
        in_specs=whole(1),
        out_specs=pl.BlockSpec(memory_space=pltpu.VMEM),
        compiler_params=VMEM,
        name=f"fold_{name}",
    )(parts)


def on_device(
    hidden, merge_weight, text_embed, gain, head_weight, owner, vis_row, lengths, labels, targets
):
    groups, near = lax.axis_size(GRP), lax.axis_size(NEAR)
    tokens, depth = hidden.shape
    positions, width = text_embed.shape
    objectives = head_weight.shape[1]
    cap = vis_row.shape[1] // groups
    features = float(width * lax.axis_size(TP))
    scale = float(positions * groups // 16)
    me = lax.axis_index(GRP).astype(jnp.int32).reshape(1)
    owners = owner.reshape(1, tokens)
    gain_row = gain.reshape(1, width)
    head = head_weight.T
    marks = labels.T

    flags = pl.pallas_call(
        functools.partial(flags_kernel, cap),
        out_shape=jax.ShapeDtypeStruct((groups, LANES), jnp.float32),
        in_specs=scalars(1) + [pl.BlockSpec(memory_space=pltpu.HBM)] * 3,
        out_specs=pl.BlockSpec(memory_space=pltpu.VMEM),
        scratch_shapes=[
            pltpu.VMEM(owners.shape, jnp.int32),
            pltpu.VMEM(vis_row.shape, jnp.int32),
            pltpu.VMEM(targets.shape, jnp.float32),
            pltpu.SemaphoreType.DMA((3,)),
        ],
        compiler_params=VMEM,
        name="flags",
    )(lengths, in_hbm(owners), in_hbm(vis_row), in_hbm(targets))
    told = lax.all_to_all(
        flags.reshape(groups, 1, LANES), GRP, split_axis=0, concat_axis=0, tiled=True
    ).reshape(groups, LANES)

    chunks = 5
    rows = tokens + positions
    visual, stats = pl.pallas_call(
        stats_kernel,
        out_shape=(
            jax.ShapeDtypeStruct((tokens, width), jnp.bfloat16),
            jax.ShapeDtypeStruct((8, 2 * rows + tight_lanes(rows)), jnp.float32),
        ),
        in_specs=[pl.BlockSpec(memory_space=pl.ANY)]
        + [pl.BlockSpec(memory_space=pltpu.HBM)] * 5,
        out_specs=tuple(whole(2)),
        scratch_shapes=[
            pltpu.VMEM((chunks, tokens, depth // chunks), jnp.bfloat16),
            pltpu.VMEM((chunks, depth // chunks, width), jnp.bfloat16),
            pltpu.VMEM((positions, width), jnp.bfloat16),
            pltpu.VMEM((K_ROWS, width), jnp.float32),
            pltpu.VMEM(gain_row.shape, jnp.float32),
            pltpu.VMEM(head.shape, jnp.float32),
            pltpu.SemaphoreType.DMA((2 * chunks + 1,)),
            pltpu.SemaphoreType.DMA((2,)),
        ],
        compiler_params=VMEM,
        name="stats",
    )(flags, in_hbm(hidden), in_hbm(merge_weight), in_hbm(text_embed), in_hbm(gain_row), in_hbm(head))
    stats = lax.all_gather(jnp.sum(lax.all_gather(stats, "tx"), axis=0), "ty")

    pooled, kept = pl.pallas_call(
        functools.partial(pooled_kernel, cap, objectives, features),
        out_shape=(
            jax.ShapeDtypeStruct((groups, width + LANES), jnp.float32),
            jax.ShapeDtypeStruct((K_ROWS, tokens), jnp.float32),
        ),
        in_specs=scalars(2) + whole(6),
        out_specs=tuple(whole(2)),
        compiler_params=VMEM,
        name="pooled",
    )(me, lengths, stats, told, owners, vis_row, visual, text_embed)
    block = pooled.reshape(near, groups // near, width + LANES)
    block = lax.all_to_all(block, NEAR, split_axis=0, concat_axis=0, tiled=True)
    block = folded(block, lax.axis_size("far"), jnp.bfloat16, "near")
    block = lax.all_to_all(block, "far", split_axis=0, concat_axis=0, tiled=True)
    block = folded(block, near, jnp.float32, "far")
    block = lax.all_to_all(block, NEAR, split_axis=0, concat_axis=0, tiled=True)
    pooled = block.reshape(groups, width + LANES)

    reward, visual_grad, head_grad, gain_grad = pl.pallas_call(
        functools.partial(grads_kernel, cap, scale),
        out_shape=(
            jax.ShapeDtypeStruct((1, LANES), jnp.float32),
            jax.ShapeDtypeStruct((tokens, width), jnp.bfloat16),
            jax.ShapeDtypeStruct((objectives, width), jnp.float32),
            jax.ShapeDtypeStruct((1, width), jnp.float32),
        ),
        in_specs=scalars(1) + whole(8),
        out_specs=tuple(whole(4)),
        scratch_shapes=[
            pltpu.VMEM((K_ROWS, groups), jnp.int32),
            pltpu.VMEM((K_ROWS, width), jnp.float32),
        ],
        compiler_params=VMEM,
        name="grads",
    )(me, pooled, kept, told, owners, visual, marks, gain_row, head)
    return reward[:, :objectives], visual_grad, head_grad.T, gain_grad.reshape(width)


def solution(mesh):
    groups, tp = mesh.shape["grp"], mesh.shape["tp"]
    near = 4 if groups % 16 == 0 else 2
    ty = 4 if tp % 16 == 0 else 1
    torus = Mesh(
        mesh.devices.reshape(groups // (2 * near), near, 2, ty, tp // ty),
        ("far", "near", "core", "ty", "tx"),
    )
    placed = (
        P(GRP, None),
        P(None, TP),
        P(GRP, TP),
        P(TP),
        P(TP, None),
        P(GRP, None),
        P(GRP, None),
        P(GRP),
        P(),
        P(GRP, None),
    )
    return jax.shard_map(
        on_device,
        mesh=torus,
        in_specs=placed,
        out_specs=(P(GRP, None), P(GRP, TP), P(TP, None), P(TP)),
        check_vma=False,
    )
```

```python
import functools

import jax
import jax.numpy as jnp
from jax import lax
from jax.experimental import pallas as pl
from jax.experimental.pallas import tpu as pltpu
from jax.sharding import Mesh
from jax.sharding import PartitionSpec as P

GRP = ("far", "near", "core")
NEAR = ("near", "core")
TP = ("ty", "tx")
EPSILON = 1e-06
LANES = 128
K_ROWS = 24
SIDE = 32
VMEM = pltpu.CompilerParams(vmem_limit_bytes=48 * 2**20)
EXACT = lax.Precision.HIGHEST
LAST = (((1,), (1,)), ((), ()))
FIRST = (((0,), (0,)), ((), ()))
ALONG = (((1,), (0,)), ((), ()))


def iota(shape, dim):
    return lax.broadcasted_iota(jnp.int32, shape, dim)


def in_three(x):
    hi = x.astype(jnp.bfloat16)
    rest = x - hi.astype(jnp.float32)
    mid = rest.astype(jnp.bfloat16)
    return hi, mid, (rest - mid.astype(jnp.float32)).astype(jnp.bfloat16)


def dot32(a, b, dims):
    return lax.dot_general(a, b, dims, preferred_element_type=jnp.float32)


def dot_exact(a, b, dims):
    return lax.dot_general(a, b, dims, precision=EXACT, preferred_element_type=jnp.float32)


def target_lane(cap):
    return -(-(cap + 2) // 8) * 8


def packed(pooled, reward):
    terms = [term.astype(jnp.float32) for term in in_three(reward)]
    terms.append(jnp.zeros((reward.shape[0], LANES - 3 * SIDE), jnp.float32))
    side = jnp.concatenate(terms, axis=1)
    return jnp.concatenate([pooled, side], axis=1).astype(jnp.bfloat16)


def rewards_of(side):
    return side[:, :SIDE] + side[:, SIDE : 2 * SIDE] + side[:, 2 * SIDE : 3 * SIDE]


def padded(ref, scratch):
    scratch[...] = jnp.zeros_like(scratch)
    scratch[: ref.shape[0]] = ref[...]
    return scratch[...]


def tight_lanes(rows):
    return -(-rows // (2 * LANES)) * LANES


def tight(stats):
    rows = stats.shape[1]
    half = tight_lanes(rows)
    last = jnp.concatenate([stats[16:20, :half], stats[16:20, rows - half :]], axis=0)
    return jnp.concatenate([stats[:8], stats[8:16], last], axis=1)


def loose(packed_stats, rows):
    half = tight_lanes(rows)
    last = packed_stats[:, 2 * rows :]
    last = jnp.concatenate([last[:4, :half], last[4:, 2 * half - rows :]], axis=1)
    last = jnp.concatenate([last, jnp.zeros_like(last)], axis=0)
    return jnp.concatenate([packed_stats[:, :rows], packed_stats[:, rows : 2 * rows], last], axis=0)


def flags_kernel(cap, length_ref, owner_ref, rows_ref, targets_ref, out_ref):
    groups = out_ref.shape[0]
    slots = rows_ref.shape[1]
    length = length_ref[0]
    live = (rows_ref[...] < length).astype(jnp.float32)
    slot = iota((groups, slots), 1)
    first = iota((groups, slots), 0) * cap
    mine = jnp.where((slot >= first) & (slot < first + cap), live, 0.0).astype(jnp.bfloat16)
    rank = lax.rem(iota((LANES, slots), 1), cap)
    place = (rank == iota((LANES, slots), 0)).astype(jnp.bfloat16)
    flags = dot32(mine, place, LAST)
    owned = (owner_ref[...] == iota((groups, owner_ref.shape[1]), 0)).astype(jnp.float32)
    count = jnp.sum(owned, axis=1, keepdims=True)
    lane = iota((groups, LANES), 1)
    flags = jnp.where(lane == cap, count, flags)
    out_ref[...] = jnp.where(lane == cap + 1, length.astype(jnp.float32), flags)
    first = target_lane(cap)
    objectives = targets_ref.shape[1]
    out_ref[:, first : first + objectives] = jnp.broadcast_to(
        targets_ref[...], (groups, objectives)
    )


def stats_kernel(
    after_ref,
    hidden_ref,
    weight_ref,
    text_ref,
    gain_hbm,
    head_hbm,
    visual_ref,
    stats_ref,
    hidden,
    weight,
    text,
    head,
    gain_ref,
    head_ref,
    arrived,
):
    chunks, tokens, depth = hidden.shape
    objectives = head_ref.shape[0]
    copies = []
    for i in range(chunks):
        part = pl.ds(i * depth, depth)
        copies.append(
            pltpu.make_async_copy(hidden_ref.at[:, part], hidden.at[i], arrived.at[2 * i])
        )
        copies.append(
            pltpu.make_async_copy(weight_ref.at[part, :], weight.at[i], arrived.at[2 * i + 1])
        )
    late = 2 * chunks
    others = [
        pltpu.make_async_copy(gain_hbm, gain_ref, arrived.at[late]),
        pltpu.make_async_copy(head_hbm, head_ref, arrived.at[late + 1]),
        pltpu.make_async_copy(text_ref, text, arrived.at[late + 2]),
    ]
    for copy in copies[:4] + others + copies[4:]:
        copy.start()

    def of_rows(gained, x):
        parts = dot32(gained, x, LAST)
        value = parts[:K_ROWS] + parts[K_ROWS : 2 * K_ROWS] + parts[2 * K_ROWS :]
        wide = x.astype(jnp.float32)
        square = wide * wide
        lanes = square[:, :LANES]
        for at in range(LANES, x.shape[1], LANES):
            lanes = lanes + square[:, at : at + LANES]
        terms = jnp.concatenate(in_three(lanes), axis=1)
        squares = dot32(jnp.ones((K_ROWS, terms.shape[1]), jnp.bfloat16), terms, LAST)
        return jnp.where(iota(value.shape, 0) == objectives, squares, value)

    total = None
    for i in range(chunks):
        copies[2 * i].wait()
        copies[2 * i + 1].wait()
        part = dot32(hidden[i], weight[i], ALONG)
        total = part if total is None else total + part
        if i == 1:
            for copy in others:
                copy.wait()
            gained = jnp.concatenate(in_three(gain_ref[...] * padded(head_ref, head)), axis=0)
            of_text = of_rows(gained, text[...])
    visual = total.astype(jnp.bfloat16)
    visual_ref[...] = visual
    stats_ref[...] = tight(jnp.concatenate([of_rows(gained, visual), of_text], axis=1))


def pooled_kernel(
    cap,
    objectives,
    features,
    me_ref,
    length_ref,
    stats_ref,
    flags_ref,
    owner_ref,
    rows_ref,
    visual_ref,
    text_ref,
    pooled_ref,
    kept_ref,
):
    tokens, width = visual_ref.shape
    positions = text_ref.shape[0]
    groups = flags_ref.shape[0]
    slots = rows_ref.shape[1]
    stats = stats_ref[0]
    for part in range(1, stats_ref.shape[0]):
        stats = stats + stats_ref[part]
    stats = loose(stats, tokens + positions)
    inv = lax.rsqrt(stats[objectives : objectives + 1] / features + EPSILON)
    flags = flags_ref[...]

    owned = owner_ref[...] == iota((groups, tokens), 0)
    member = owned.astype(jnp.bfloat16)
    before = (iota((tokens, tokens), 0) < iota((tokens, tokens), 1)).astype(jnp.bfloat16)
    earlier = dot32(member, before, ALONG)
    rank = jnp.sum(jnp.where(owned, earlier, 0.0), axis=0, keepdims=True)
    told = dot_exact(flags, owned.astype(jnp.float32), FIRST)
    at = iota(told.shape, 0)
    live = jnp.sum(
        jnp.where((at < cap) & (at == rank.astype(jnp.int32)), told, 0.0), axis=0, keepdims=True
    )
    token_inv = inv[:, :tokens]
    token_weight = live * token_inv / told[cap + 1 : cap + 2]

    length = length_ref[0]
    slot = iota((groups, slots), 1)
    first = iota((groups, slots), 0) * cap
    count = flags[:, cap : cap + 1].astype(jnp.int32)
    used = jnp.sum(((slot >= first) & (slot < first + count)).astype(jnp.float32), axis=0, keepdims=True)
    row = rows_ref[...]
    tall = positions // LANES
    high = jnp.where(lax.div(row, LANES) == iota((tall, slots), 0), used, 0.0).astype(jnp.bfloat16)
    low = (lax.rem(row, LANES) == iota((LANES, slots), 0)).astype(jnp.bfloat16)
    replaced = dot32(high, low, LAST)
    replaced = jnp.concatenate([replaced[i : i + 1] for i in range(tall)], axis=1)
    stays = (iota((1, positions), 1) < length) & (replaced < 0.5)
    text_weight = jnp.where(stays, inv[:, tokens:], 0.0) / length.astype(jnp.float32)

    spread = jnp.where(owned, token_weight, 0.0)
    three = dot32(jnp.concatenate(in_three(spread), axis=0), visual_ref[...], ALONG)
    pooled = three[:groups] + three[groups : 2 * groups] + three[2 * groups :]
    reward = dot_exact(spread, stats[:, :tokens], LAST)
    split = jnp.concatenate(in_three(jnp.broadcast_to(text_weight, (16, positions))), axis=0)
    text_three = dot32(split, text_ref[...], ALONG)
    text_pooled = text_three[0:1] + text_three[16:17] + text_three[32:33]
    text_reward = dot_exact(
        jnp.broadcast_to(text_weight, (8, positions)), stats[:, tokens:], LAST
    )[0:1]
    mine = iota((groups, 1), 0) == me_ref[0]
    pooled_ref[:, :width] = pooled + jnp.where(mine, text_pooled, 0.0)
    reward = reward + jnp.where(mine, text_reward, 0.0)
    pooled_ref[:, width:] = jnp.zeros((groups, LANES), jnp.float32)
    pooled_ref[:, width : width + objectives] = reward[:, :objectives]
    kept = jnp.where(iota((K_ROWS, tokens), 0) == objectives, token_weight, stats[:, :tokens])
    factor = token_weight * token_inv * token_inv / features
    kept_ref[...] = jnp.where(iota((K_ROWS, tokens), 0) == objectives + 1, factor, kept)


def fold_kernel(parts_ref, out_ref):
    total = parts_ref[0].astype(jnp.float32)
    for part in range(1, parts_ref.shape[0]):
        total = total + parts_ref[part].astype(jnp.float32)
    width = total.shape[1] - LANES
    joined, side = total[:, :width], total[:, width:]
    if out_ref.dtype == jnp.bfloat16:
        once = packed(joined, side[:, :SIDE])
    else:
        spare = jnp.zeros((side.shape[0], LANES - SIDE), jnp.float32)
        once = jnp.concatenate([joined, rewards_of(side), spare], axis=1)
    for copy in range(out_ref.shape[0]):
        out_ref[copy] = once


def grads_kernel(
    cap,
    scale,
    me_ref,
    pooled_ref,
    kept_ref,
    flags_ref,
    owner_ref,
    visual_ref,
    labels_ref,
    gain_ref,
    head_ref,
    reward_ref,
    visual_grad_ref,
    head_grad_ref,
    gain_grad_ref,
    marks,
    head_all,
):
    tokens, width = visual_ref.shape
    groups = flags_ref.shape[0]
    objectives = labels_ref.shape[0]
    z = pooled_ref[:, :width]
    rest = pooled_ref[:, width:]
    mine = iota(rest.shape, 0) == me_ref[0]
    reward_ref[...] = jnp.sum(jnp.where(mine, rest, 0.0), axis=0, keepdims=True)
    first = target_lane(cap)
    error = rest.T[:K_ROWS] - flags_ref[...].T[first : first + K_ROWS]
    labels = padded(labels_ref, marks).astype(jnp.float32)
    count = jnp.maximum(jnp.sum(labels, axis=1, keepdims=True), 1.0)
    cot = scale * labels * error / count
    gain = gain_ref[...]
    head = padded(head_ref, head_all)
    head_grad_ref[...] = (gain * dot_exact(cot, z, ALONG))[:objectives]
    direction = dot_exact(cot, head, FIRST)
    gain_grad_ref[...] = jnp.sum(z * direction, axis=0, keepdims=True)
    owned = owner_ref[...] == iota((groups, tokens), 0)
    kept = kept_ref[...]
    own_cot = dot_exact(cot, owned.astype(jnp.float32), ALONG)
    is_value = iota(kept.shape, 0) < objectives
    row_dot = jnp.sum(jnp.where(is_value, kept * own_cot, 0.0), axis=0, keepdims=True)
    weight = kept[objectives : objectives + 1]
    beta = kept[objectives + 1 : objectives + 2] * row_dot
    both = jnp.concatenate([weight, beta, jnp.zeros((LANES - 2, tokens), jnp.float32)], axis=0)
    columns = both.T
    member = owned.astype(jnp.bfloat16)
    directions = jnp.concatenate(in_three(gain * direction), axis=0)
    own = dot32(jnp.concatenate([member] * 3, axis=0), directions, FIRST)
    grad = columns[:, 0:1] * own - columns[:, 1:2] * visual_ref[...].astype(jnp.float32)
    visual_grad_ref[...] = grad.astype(jnp.bfloat16)


def whole(count):
    return [pl.BlockSpec(memory_space=pltpu.VMEM)] * count


def in_hbm(array):
    return pltpu.with_memory_space_constraint(array, pltpu.HBM)


def scalars(count):
    return [pl.BlockSpec(memory_space=pltpu.SMEM)] * count


def folded(parts, copies, kind, name):
    return pl.pallas_call(
        fold_kernel,
        out_shape=jax.ShapeDtypeStruct((copies, *parts.shape[1:]), kind),
        in_specs=whole(1),
        out_specs=pl.BlockSpec(memory_space=pltpu.VMEM),
        compiler_params=VMEM,
        name=f"fold_{name}",
    )(parts)


def on_device(
    hidden, merge_weight, text_embed, gain, head_weight, owner, vis_row, lengths, labels, targets
):
    groups, near = lax.axis_size(GRP), lax.axis_size(NEAR)
    tokens, depth = hidden.shape
    positions, width = text_embed.shape
    objectives = head_weight.shape[1]
    cap = vis_row.shape[1] // groups
    features = float(width * lax.axis_size(TP))
    scale = float(positions * groups // 16)
    me = lax.axis_index(GRP).astype(jnp.int32).reshape(1)
    owners = owner.reshape(1, tokens)
    gain_row = gain.reshape(1, width)
    head = head_weight.T
    marks = labels.T

    flags = pl.pallas_call(
        functools.partial(flags_kernel, cap),
        out_shape=jax.ShapeDtypeStruct((groups, LANES), jnp.float32),
        in_specs=scalars(1) + whole(3),
        out_specs=pl.BlockSpec(memory_space=pltpu.VMEM),
        compiler_params=VMEM,
        name="flags",
    )(lengths, in_hbm(owners), in_hbm(vis_row), in_hbm(targets))
    told = lax.all_to_all(
        flags.reshape(groups, 1, LANES), GRP, split_axis=0, concat_axis=0, tiled=True
    ).reshape(groups, LANES)

    chunks = 5
    rows = tokens + positions
    visual, stats = pl.pallas_call(
        stats_kernel,
        out_shape=(
            jax.ShapeDtypeStruct((tokens, width), jnp.bfloat16),
            jax.ShapeDtypeStruct((8, 2 * rows + tight_lanes(rows)), jnp.float32),
        ),
        in_specs=[pl.BlockSpec(memory_space=pl.ANY)]
        + [pl.BlockSpec(memory_space=pltpu.HBM)] * 5,
        out_specs=tuple(whole(2)),
        scratch_shapes=[
            pltpu.VMEM((chunks, tokens, depth // chunks), jnp.bfloat16),
            pltpu.VMEM((chunks, depth // chunks, width), jnp.bfloat16),
            pltpu.VMEM((positions, width), jnp.bfloat16),
            pltpu.VMEM((K_ROWS, width), jnp.float32),
            pltpu.VMEM(gain_row.shape, jnp.float32),
            pltpu.VMEM(head.shape, jnp.float32),
            pltpu.SemaphoreType.DMA((2 * chunks + 3,)),
        ],
        compiler_params=VMEM,
        name="stats",
    )(flags, in_hbm(hidden), in_hbm(merge_weight), in_hbm(text_embed), in_hbm(gain_row), in_hbm(head))
    stats = lax.all_gather(jnp.sum(lax.all_gather(stats, "tx"), axis=0), "ty")

    pooled, kept = pl.pallas_call(
        functools.partial(pooled_kernel, cap, objectives, features),
        out_shape=(
            jax.ShapeDtypeStruct((groups, width + LANES), jnp.float32),
            jax.ShapeDtypeStruct((K_ROWS, tokens), jnp.float32),
        ),
        in_specs=scalars(2) + whole(6),
        out_specs=tuple(whole(2)),
        compiler_params=VMEM,
        name="pooled",
    )(me, lengths, stats, told, owners, vis_row, visual, text_embed)
    block = pooled.reshape(near, groups // near, width + LANES)
    block = lax.all_to_all(block, NEAR, split_axis=0, concat_axis=0, tiled=True)
    block = folded(block, lax.axis_size("far"), jnp.bfloat16, "near")
    block = lax.all_to_all(block, "far", split_axis=0, concat_axis=0, tiled=True)
    block = folded(block, near, jnp.float32, "far")
    block = lax.all_to_all(block, NEAR, split_axis=0, concat_axis=0, tiled=True)
    pooled = block.reshape(groups, width + LANES)

    reward, visual_grad, head_grad, gain_grad = pl.pallas_call(
        functools.partial(grads_kernel, cap, scale),
        out_shape=(
            jax.ShapeDtypeStruct((1, LANES), jnp.float32),
            jax.ShapeDtypeStruct((tokens, width), jnp.bfloat16),
            jax.ShapeDtypeStruct((objectives, width), jnp.float32),
            jax.ShapeDtypeStruct((1, width), jnp.float32),
        ),
        in_specs=scalars(1) + whole(8),
        out_specs=tuple(whole(4)),
        scratch_shapes=[
            pltpu.VMEM((K_ROWS, groups), jnp.int32),
            pltpu.VMEM((K_ROWS, width), jnp.float32),
        ],
        compiler_params=VMEM,
        name="grads",
    )(me, pooled, kept, told, owners, visual, marks, gain_row, head)
    return reward[:, :objectives], visual_grad, head_grad.T, gain_grad.reshape(width)


def solution(mesh):
    groups, tp = mesh.shape["grp"], mesh.shape["tp"]
    near = 4 if groups % 16 == 0 else 2
    ty = 4 if tp % 16 == 0 else 1
    torus = Mesh(
        mesh.devices.reshape(groups // (2 * near), near, 2, ty, tp // ty),
        ("far", "near", "core", "ty", "tx"),
    )
    placed = (
        P(GRP, None),
        P(None, TP),
        P(GRP, TP),
        P(TP),
        P(TP, None),
        P(GRP, None),
        P(GRP, None),
        P(GRP),
        P(),
        P(GRP, None),
    )
    return jax.shard_map(
        on_device,
        mesh=torus,
        in_specs=placed,
        out_specs=(P(GRP, None), P(GRP, TP), P(TP, None), P(TP)),
        check_vma=False,
    )
```
